256 devices in a mesh: wide: 64 (over z, x_hi, y), narrow: 4 (over x_lo, core).
Axes of the slice: x: 4 (x_hi: 2, x_lo: 2; x = x_hi * 2 + x_lo), y: 4, z: 8, core: 2. Of those that a mesh axis runs over, the one named last changes fastest.
Arguments:
- amplitudes: float32 [1536, 32768], P('narrow', 'wide'), may hold values from -6 to 6
- integrals: float32 [512, 64, 64, 64], P('wide', 'narrow'), may hold values from -0.09375 to 0.09375
- send_tiles: int32 [64, 64], P('wide'), may hold values from 0 to 7
- task_slots: int32 [512, 64], P('wide'), may hold values from 0 to 63, as said below
- row_gap: float32 [32768], P('wide'), may hold values from 0.5 to 4
- column_gap: float32 [1536], P('narrow'), may hold values from 0.5 to 4
Outputs:
- residual: float32 [1536, 32768], P('narrow', 'wide')
- new_amplitudes: float32 [1536, 32768], P('narrow', 'wide')
The draws below stay inside these ranges and needn't reach their ends.
Inputs may be any that keep to these rules, and one draw needn't show every extreme that they name: `task_slots`: within each row tile the 64 entries are distinct; among the 8 row tiles of one owner every wide index is named exactly 8 times.
All inputs are finite; a program needn't handle non-finite values.
Results may differ from the reference program's by a relative error of at most 0.0003.
Values sent between devices are 32-bit elements; how exact they have to be, the bound alone decides.
No kernel may reach another device: no remote copies, remote signals or barrier semaphores. Data moves between devices by JAX's collectives and lax.ppermute only.
A program may use at most 128 MiB of HBM per device.

```python
import math
import jax
import jax.numpy as jnp
from jax import lax

TILE = 64
TILE_DEV = 8
TERMS = 64
TILES = 512
ROWS = 32768
COLUMNS = 1536
N_WIDE = 64


def draw_task_slots(key, part):
    key = jax.random.fold_in(key, 11)
    keys = jax.random.split(key, N_WIDE)

    def owner_slots(owner_key):
        first_key, second_key = jax.random.split(owner_key)
        order = jax.random.permutation(first_key, N_WIDE)
        row_order = jax.random.permutation(second_key, TILE_DEV)
        starts = row_order * N_WIDE // TILE_DEV
        position = (starts[:, None] + jnp.arange(TERMS)[None, :]) % N_WIDE
        return order[position]
    return jax.vmap(owner_slots)(keys).reshape(TILES, TERMS).astype(jnp.int32)


def set_ends(entries, stream_key, low, high):
    shape = entries.shape
    spot = [jax.random.randint(jax.random.fold_in(stream_key, axis), (), 0, shape[axis]) for axis in range(len(shape))]
    entries = entries.at[tuple(spot)].set(low)
    longest = shape.index(max(shape))
    spot[longest] = (spot[longest] + 1) % shape[longest]
    return entries.at[tuple(spot)].set(high)


def block_levels(rng, extent, pieces, low, top_value):
    def one(dim, shards_of):
        draws = jax.random.uniform(jax.random.fold_in(jax.random.fold_in(rng, 6), dim), (shards_of,), jnp.float32, low / len(pieces), top_value / len(pieces))
        return jnp.repeat(jnp.exp(draws), extent[dim] // shards_of).reshape((-1,) + (1,) * (len(extent) - dim - 1))

    gain = one(*pieces[0])
    for cut in pieces[1:]:
        gain = gain * one(*cut)
    return gain


def noise(rng, shape, scale, most, cuts=(), kind=jnp.bfloat16):
    result = scale * jax.random.normal(rng, shape, jnp.float32)
    if cuts:
        result = result * block_levels(rng, shape, cuts, -0.22, 0.18)
    return jnp.clip(result, -most, most).astype(kind)


def setup_inputs(seed: int = 0) -> dict:
    seeds = jax.random.split(jax.random.key(seed), 7)
    amplitudes = noise(seeds[0], (COLUMNS, ROWS), 1.0, 6.0, ((0, 4), (1, 64)), jnp.float32)
    integrals = noise(seeds[1], (TILES, TERMS, TILE, TILE), (TERMS * TILE) ** -0.5, 0.09375, ((0, 64), (1, 4)), jnp.float32)
    send_tiles = set_ends(jax.random.randint(seeds[2], (N_WIDE, N_WIDE), 0, TILE_DEV), jax.random.fold_in(seeds[2], 1), 0, TILE_DEV - 1).astype(jnp.int32)
    task_slots = draw_task_slots(jax.random.fold_in(seeds[6], 71), 0)
    row_gap = jnp.clip(jnp.exp(math.log(4.0) - 2.0794415 * jax.random.uniform(seeds[4], (ROWS,), jnp.float32) ** block_levels(seeds[4], (ROWS,), ((0, 64),), -0.2, 0.2)), 0.5, 4.0)
    column_gap = jnp.clip(jnp.exp(math.log(4.0) - 2.0794415 * jax.random.uniform(seeds[5], (COLUMNS,), jnp.float32) ** block_levels(seeds[5], (COLUMNS,), ((0, 4),), -0.2, 0.2)), 0.5, 4.0)
    return dict(amplitudes=amplitudes, integrals=integrals, send_tiles=send_tiles, task_slots=task_slots, row_gap=row_gap, column_gap=column_gap)


def reference(amplitudes, integrals, send_tiles, task_slots, row_gap, column_gap):
    tiles = amplitudes.reshape(COLUMNS, TILES, TILE)
    owners = (jnp.arange(TILES, dtype=jnp.int32) // TILE_DEV).astype(jnp.int32)

    def tile_cycle(inputs):
        owner_index, sources, integral_rows = inputs
        source_tile = (sources * TILE_DEV + send_tiles[sources, owner_index]).astype(jnp.int32)
        picked = tiles[:, source_tile, :]
        return jnp.einsum("ckv,kuv->cu", picked, integral_rows, precision=lax.Precision.HIGHEST)

    cycle = lax.map(tile_cycle, (owners, task_slots, integrals))
    cycle = jnp.transpose(cycle, (1, 0, 2)).reshape(COLUMNS, ROWS)
    gap = column_gap[:, None] + row_gap[None, :]
    residual = cycle - gap * amplitudes
    new_amplitudes = amplitudes + residual / gap
    return residual, new_amplitudes
```

```python
import jax
import jax.numpy as jnp
from jax import lax
from jax.experimental import pallas as pl
from jax.experimental.pallas import tpu as pltpu
from jax.sharding import Mesh, PartitionSpec as P

OWNERS = 64
TILE = 64
ROW_TILES = 8
TERM_SHARE = 16
GROUP = 4


def split(x):
    hi = x.astype(jnp.bfloat16)
    lo = (x - hi.astype(jnp.float32)).astype(jnp.bfloat16)
    return hi, lo


def contract_kernel(spot, tiles, i0, i1, i2, i3, amp, row_gap, col_gap, res, new, held, src, acc, lhs_hi, lhs_lo, isem, asem):
    pieces = (i0, i1, i2, i3)
    per = ROW_TILES * TERM_SHARE
    icopies = [pltpu.make_async_copy(p, held.at[pl.ds(n * per, per)], isem.at[n]) for n, p in enumerate(pieces)]
    acopy = pltpu.make_async_copy(tiles, src, asem)
    for c in icopies:
        c.start()
    acopy.start()
    acc[...] = jnp.zeros_like(acc)
    low = lax.broadcasted_iota(jnp.int32, (TILE // 2, 2 * TILE), 1) < TILE
    for c in icopies:
        c.wait()
    acopy.wait()

    def step(g, carry):
        for x in range(ROW_TILES):
            for pair in range(GROUP // 2):
                s = g * GROUP + 2 * pair
                first = held[spot[x, s]]
                second = held[spot[x, s + 1]]
                top = jnp.where(low, first, pltpu.roll(second, TILE, 1))
                bottom = jnp.where(low, pltpu.roll(first, TILE, 1), second)
                for half, value in enumerate((top, bottom)):
                    hi, lo = split(value)
                    rows = pl.ds(x * TILE + half * (TILE // 2), TILE // 2)
                    cols = pl.ds(pair * 2 * TILE, 2 * TILE)
                    lhs_hi[rows, cols] = hi
                    lhs_lo[rows, cols] = lo
        block = src[pl.ds(g * GROUP, GROUP)].reshape(GROUP * TILE, src.shape[2])
        hi, lo = split(block)
        left_hi, left_lo = lhs_hi[...], lhs_lo[...]
        total = jnp.dot(left_hi, lo, preferred_element_type=jnp.float32)
        total += jnp.dot(left_lo, hi, preferred_element_type=jnp.float32)
        total += jnp.dot(left_hi, hi, preferred_element_type=jnp.float32)
        acc[...] += total
        return carry

    lax.fori_loop(0, OWNERS // GROUP, step, 0)
    cycle = acc[...].T
    column = jnp.broadcast_to(col_gap[...], (8, col_gap.shape[1])).T[:, :1]
    gap = column + row_gap[...]
    amplitudes = amp[...]
    residual = cycle - gap * amplitudes
    res[...] = residual
    new[...] = amplitudes + residual / gap


def contract(spot, tiles, pieces, amp, row_gap, col_gap):
    cols, rows = amp.shape
    shape = jax.ShapeDtypeStruct((cols, rows), jnp.float32)
    anywhere = pl.BlockSpec(memory_space=pl.ANY)
    inside = pl.BlockSpec(memory_space=pltpu.VMEM)
    return pl.pallas_call(
        contract_kernel,
        out_shape=(shape, shape),
        in_specs=[pl.BlockSpec(memory_space=pltpu.SMEM)] + [anywhere] * 5 + [inside] * 3,
        out_specs=(inside, inside),
        scratch_shapes=[
            pltpu.VMEM((4 * ROW_TILES * TERM_SHARE, TILE // 2, 2 * TILE), jnp.float32),
            pltpu.VMEM((OWNERS, TILE, cols), jnp.float32),
            pltpu.VMEM((rows, cols), jnp.float32),
            pltpu.VMEM((rows, GROUP * TILE), jnp.bfloat16),
            pltpu.VMEM((rows, GROUP * TILE), jnp.bfloat16),
            pltpu.SemaphoreType.DMA((4,)),
            pltpu.SemaphoreType.DMA,
        ],
        compiler_params=pltpu.CompilerParams(vmem_limit_bytes=48 * 1024 * 1024),
    )(spot, tiles, *pieces, amp, row_gap, col_gap)


def swap(x, axis):
    return lax.ppermute(x, axis, [(0, 1), (1, 0)])


def body(amplitudes, integrals, send_tiles, task_slots, row_gap, column_gap):
    cols, rows = amplitudes.shape
    packed = jnp.concatenate([integrals[:, :, : TILE // 2], integrals[:, :, TILE // 2 :]], axis=3)
    packed = packed.reshape(ROW_TILES * TERM_SHARE, TILE // 2, 2 * TILE)
    across = swap(packed, "xl")
    beside = swap(packed, "co")
    diagonal = swap(across, "co")
    owned = amplitudes.T.reshape(ROW_TILES, TILE, cols)
    outgoing = owned.at[send_tiles[0]].get(mode="promise_in_bounds")
    received = lax.all_to_all(outgoing, ("z", "xh", "y"), 0, 0, tiled=True)
    mine = lax.axis_index("xl") * 2 + lax.axis_index("co")
    names = jnp.arange(OWNERS, dtype=jnp.int32)
    term = jnp.sum(jnp.where(task_slots[:, None, :] == names[None, :, None], names[None, None, :], 0), axis=2)
    relative = (term // TERM_SHARE) ^ mine
    spot = (relative * ROW_TILES + jnp.arange(ROW_TILES, dtype=jnp.int32)[:, None]) * TERM_SHARE + term % TERM_SHARE
    return contract(spot, received, (packed, beside, across, diagonal), amplitudes, row_gap[None, :], column_gap[None, :])


def solution(mesh):
    fine = Mesh(mesh.devices.reshape(8, 2, 4, 2, 2), ("z", "xh", "y", "xl", "co"))
    wide, narrow = ("z", "xh", "y"), ("xl", "co")
    return jax.shard_map(
        body,
        mesh=fine,
        in_specs=(P(narrow, wide), P(wide, narrow, None, None), P(wide, None), P(wide, None), P(wide), P(narrow)),
        out_specs=(P(narrow, wide), P(narrow, wide)),
        check_vma=False,
    )
```

```python
import functools

import jax
import jax.numpy as jnp
from jax import lax
from jax.experimental import pallas as pl
from jax.experimental.pallas import tpu as pltpu
from jax.sharding import Mesh, PartitionSpec as P

Z, XH, Y, XL, CO = 8, 2, 4, 2, 2
PLANE = XH * Y
OWNERS = Z * PLANE
TILE = 64
ROW_TILES = 8
TERM_SHARE = 16
GROUP = 4
STEPS = ((1, -1), (2, -2), (3, -3), (0,), (4,))
MIRRORED = (True, True, True, True, False)
ANYWHERE = pl.BlockSpec(memory_space=pl.ANY)
INSIDE = pl.BlockSpec(memory_space=pltpu.VMEM)
SCALARS = pl.BlockSpec(memory_space=pltpu.SMEM)
PARAMS = pltpu.CompilerParams(vmem_limit_bytes=40 * 1024 * 1024)


def split(x):
    hi = x.astype(jnp.bfloat16)
    lo = (x - hi.astype(jnp.float32)).astype(jnp.bfloat16)
    return hi, lo


def select_kernel(parts, choice, *refs):
    sources, out, sems = refs[:-2], refs[-2], refs[-1]
    held = ROW_TILES // parts
    copies = []
    for dest in range(PLANE):
        for n in range(out.shape[1]):
            tile = choice[n, dest]
            target, sem = out.at[dest, n], sems.at[n * PLANE + dest]
            if parts == 1:
                copy = pltpu.make_async_copy(sources[n].at[tile], target, sem)
                copy.start()
                copies.append(copy)
            else:
                lower = pltpu.make_async_copy(sources[0].at[jnp.minimum(tile, held - 1)], target, sem)
                upper = pltpu.make_async_copy(sources[1].at[jnp.maximum(tile - held, 0)], target, sem)
                pl.when(tile < held)(lower.start)
                pl.when(tile >= held)(upper.start)
                copies.append(lower)
    for copy in copies:
        copy.wait()


def select(choice, sources, parts=1):
    owners = len(sources) // parts
    return pl.pallas_call(
        functools.partial(select_kernel, parts),
        out_shape=jax.ShapeDtypeStruct((PLANE, owners) + sources[0].shape[1:], jnp.float32),
        in_specs=[SCALARS] + [ANYWHERE] * len(sources),
        out_specs=ANYWHERE,
        scratch_shapes=[pltpu.SemaphoreType.DMA((PLANE * owners,))],
    )(choice, *sources)


def prepare_kernel(spot, i0, i1, i2, i3, out_hi, out_lo, held, sems):
    per = ROW_TILES * TERM_SHARE
    g = pl.program_id(0)

    @pl.when(g == 0)
    def _():
        copies = [
            pltpu.make_async_copy(piece, held.at[pl.ds(n * per, per)], sems.at[n])
            for n, piece in enumerate((i0, i1, i2, i3))
        ]
        for copy in copies:
            copy.start()
        for copy in copies:
            copy.wait()

    low = lax.broadcasted_iota(jnp.int32, (TILE // 2, 2 * TILE), 1) < TILE
    for x in range(ROW_TILES):
        for pair in range(GROUP // 2):
            s = g * GROUP + 2 * pair
            first = held[spot[x, s]]
            second = held[spot[x, s + 1]]
            top = jnp.where(low, first, pltpu.roll(second, TILE, 1))
            bottom = jnp.where(low, pltpu.roll(first, TILE, 1), second)
            for half, value in enumerate((top, bottom)):
                hi, lo = split(value)
                rows = pl.ds(x * TILE + half * (TILE // 2), TILE // 2)
                cols = pl.ds(pair * 2 * TILE, 2 * TILE)
                out_hi[rows, cols] = hi
                out_lo[rows, cols] = lo


def prepare(spot, pieces):
    rows, width = ROW_TILES * TILE, GROUP * TILE
    shape = jax.ShapeDtypeStruct((rows, OWNERS * TILE), jnp.bfloat16)
    block = pl.BlockSpec((rows, width), lambda g: (0, g))
    return pl.pallas_call(
        prepare_kernel,
        grid=(OWNERS // GROUP,),
        out_shape=(shape, shape),
        in_specs=[SCALARS] + [ANYWHERE] * 4,
        out_specs=(block, block),
        scratch_shapes=[
            pltpu.VMEM((4 * ROW_TILES * TERM_SHARE, TILE // 2, 2 * TILE), jnp.float32),
            pltpu.SemaphoreType.DMA((4,)),
        ],
        compiler_params=PARAMS,
    )(spot, *pieces)


def product(left_hi, left_lo, right):
    hi, lo = split(right)
    total = jnp.dot(left_hi, lo, preferred_element_type=jnp.float32)
    total += jnp.dot(left_lo, hi, preferred_element_type=jnp.float32)
    return total + jnp.dot(left_hi, hi, preferred_element_type=jnp.float32)


def step_kernel(mirrored, has_total, half, tiles, left_hi, left_lo, *refs):
    out = refs[-1]
    if has_total:
        out[...] = refs[0][...]
    else:
        out[...] = jnp.zeros_like(out)
    depth = left_hi.shape[1] // XH
    values = tiles[...].reshape(XH, depth, tiles.shape[-1])
    for xh in range(XH):
        part = pl.ds(xh * depth, depth)
        which = half[0] ^ xh if mirrored else 0
        out[which] += product(left_hi[:, part], left_lo[:, part], values[xh])


def step(mirrored, index, half, tiles, left, total):
    rows, cols = left[0].shape[0], tiles.shape[-1]
    depth = PLANE * tiles.shape[1] * TILE
    shape = jax.ShapeDtypeStruct((2, rows, cols), jnp.float32)
    block = pl.BlockSpec((rows, depth), lambda g: (0, index))
    whole = pl.BlockSpec((2, rows, cols), lambda g: (0, 0, 0))
    tile_block = pl.BlockSpec(tiles.shape, lambda g: (0, 0, 0, 0))
    has_total = total is not None
    return pl.pallas_call(
        functools.partial(step_kernel, mirrored, has_total),
        grid=(1,),
        out_shape=shape,
        in_specs=[SCALARS, tile_block, block, block] + [whole] * has_total,
        out_specs=whole,
        compiler_params=PARAMS,
    )(half, tiles, *left, *([total] if has_total else []))


def last_kernel(tiles, left_hi, left_lo, total, other, amp, row_gap, col_gap, res, new):
    values = tiles[...].reshape(left_hi.shape[1], tiles.shape[-1])
    cycle = (total[0] + other[...] + product(left_hi[...], left_lo[...], values)).T
    column = jnp.broadcast_to(col_gap[...], (8, col_gap.shape[1])).T[:, :1]
    gap = column + row_gap[...]
    amplitudes = amp[...]
    residual = cycle - gap * amplitudes
    res[...] = residual
    new[...] = amplitudes + residual / gap


def last(index, tiles, left, total, other, amp, row_gap, col_gap):
    rows, cols = left[0].shape[0], tiles.shape[-1]
    depth = PLANE * tiles.shape[1] * TILE
    shape = jax.ShapeDtypeStruct((cols, rows), jnp.float32)
    block = pl.BlockSpec((rows, depth), lambda g: (0, index))

    def full(x):
        return pl.BlockSpec(x.shape, lambda g: (0,) * x.ndim)

    return pl.pallas_call(
        last_kernel,
        grid=(1,),
        out_shape=(shape, shape),
        in_specs=[full(tiles), block, block, pl.BlockSpec((1, rows, cols), lambda g: (0, 0, 0)), full(other), full(amp), full(row_gap), full(col_gap)],
        out_specs=(full(shape), full(shape)),
        compiler_params=PARAMS,
    )(tiles, *left, total, other, amp, row_gap, col_gap)


def swap(x, axis):
    return lax.ppermute(x, axis, [(0, 1), (1, 0)])


def shift(x, by):
    return lax.ppermute(x, "z", [(i, (i + by) % Z) for i in range(Z)])


def exchange(x, mirrored):
    if not mirrored:
        return lax.all_to_all(x, ("xh", "y"), 0, 0, tiled=True)
    groups = [[(xh * Y + y) * XL + (xh ^ d) for xh in range(XH) for y in range(Y)] for d in range(XL)]
    return lax.all_to_all(x, ("xh", "y", "xl"), 0, 0, axis_index_groups=groups, tiled=True)


def body(amplitudes, integrals, send_tiles, task_slots, row_gap, column_gap):
    cols, rows = amplitudes.shape
    z, half = lax.axis_index("z"), lax.axis_index("xh")
    half = half[None].astype(jnp.int32)

    owned = amplitudes.T.reshape(ROW_TILES, TILE, cols)
    packed = jnp.concatenate([integrals[:, :, : TILE // 2], integrals[:, :, TILE // 2 :]], axis=3)
    packed = packed.reshape(ROW_TILES * TERM_SHARE, TILE // 2, 2 * TILE)
    across = swap(packed, "xl")
    beside = swap(packed, "co")
    diagonal = swap(across, "co")

    asked = lax.all_gather(send_tiles[0].reshape(Z, PLANE), "z", axis=0)
    asked = lax.dynamic_index_in_dim(asked, z, 1, keepdims=False)

    held = ROW_TILES // 2
    ring = {0: owned}
    for t in range(1, Z // 2):
        ring[-t] = shift(ring[1 - t], 1)
        ring[t] = shift(ring[t - 1], -1)
    far = (shift(ring[1 - Z // 2][:held], 1), shift(ring[Z // 2 - 1][held:], -1))

    order, received = [], []
    for offsets, mirrored in zip(STEPS, MIRRORED):
        places = (z + jnp.array(offsets, jnp.int32)) % Z
        choice = asked[places]
        sources = far if offsets == (Z // 2,) else [ring[o] for o in offsets]
        outgoing = select(choice, sources, len(sources) // len(offsets))
        received.append(exchange(outgoing, mirrored))
        order.append((places[None, :] * PLANE + jnp.arange(PLANE, dtype=jnp.int32)[:, None]).reshape(-1))
    order = jnp.concatenate(order)

    mine = lax.axis_index("xl") * CO + lax.axis_index("co")
    terms = jnp.arange(OWNERS, dtype=jnp.int32)
    term = jnp.sum(jnp.where(task_slots[:, None, :] == order[None, :, None], terms[None, None, :], 0), axis=2)
    relative = (term // TERM_SHARE) ^ mine
    spot = (relative * ROW_TILES + jnp.arange(ROW_TILES, dtype=jnp.int32)[:, None]) * TERM_SHARE + term % TERM_SHARE
    left = prepare(spot, (packed, beside, across, diagonal))

    total = None
    for n, index in ((3, 6), (0, 0), (1, 1), (2, 2)):
        total = step(MIRRORED[n], index, half, received[n], left, total)
    other = swap(total[1], "xl")
    return last(7, received[4], left, total, other, amplitudes, row_gap[None, :], column_gap[None, :])


def solution(mesh):
    fine = Mesh(mesh.devices.reshape(Z, XH, Y, XL, CO), ("z", "xh", "y", "xl", "co"))
    wide, narrow = ("z", "xh", "y"), ("xl", "co")
    return jax.shard_map(
        body,
        mesh=fine,
        in_specs=(P(narrow, wide), P(wide, narrow, None, None), P(wide, None), P(wide, None), P(wide), P(narrow)),
        out_specs=(P(narrow, wide), P(narrow, wide)),
        check_vma=False,
    )
```

```python
import functools

import jax
import jax.numpy as jnp
from jax import lax
from jax.experimental import pallas as pl
from jax.experimental.pallas import tpu as pltpu
from jax.sharding import Mesh, PartitionSpec as P

Z, XH, Y, XL, CO = 8, 2, 4, 2, 2
PLANE = XH * Y
OWNERS = Z * PLANE
TILE = 64
ROW_TILES = 8
TERM_SHARE = 16
GROUP = 4
NOTE = 8
SELECT_COST = 40
STEPS = ((0,), (1, -1), (2, -2), (3, -3, 4))
MIRRORED = (True, True, True, False)
ANYWHERE = pl.BlockSpec(memory_space=pl.ANY)
IN_HBM = pl.BlockSpec(memory_space=pltpu.HBM)
INSIDE = pl.BlockSpec(memory_space=pltpu.VMEM)
SCALARS = pl.BlockSpec(memory_space=pltpu.SMEM)
PARAMS = pltpu.CompilerParams(vmem_limit_bytes=40 * 1024 * 1024)


def cost(micros):
    return pl.CostEstimate(flops=int(micros * 1e9), bytes_accessed=0, transcendentals=0)


def in_hbm(*xs):
    return [pltpu.with_memory_space_constraint(x, pltpu.HBM) for x in xs]


def split(x):
    hi = x.astype(jnp.bfloat16)
    lo = (x - hi.astype(jnp.float32)).astype(jnp.bfloat16)
    return hi, lo


def first_kernel(amp, send, out, held, sem):
    rows = amp.shape[1]
    held[pl.ds(0, rows)] = amp[...].T
    wide = jnp.pad(send[...].astype(jnp.float32), ((0, 0), (0, amp.shape[0] - OWNERS)))
    held[pl.ds(rows, NOTE)] = jnp.broadcast_to(wide, (NOTE, amp.shape[0]))
    copy = pltpu.make_async_copy(held, out, sem)
    copy.start()
    copy.wait()


def first(amp, send):
    cols, rows = amp.shape
    return pl.pallas_call(
        first_kernel,
        out_shape=jax.ShapeDtypeStruct((rows + NOTE, cols), jnp.float32),
        in_specs=[INSIDE, INSIDE],
        out_specs=IN_HBM,
        scratch_shapes=[pltpu.VMEM((rows + NOTE, cols), jnp.float32), pltpu.SemaphoreType.DMA],
    )(amp, send)


def select_kernel(base, *refs):
    owners = (len(refs) - 3)
    sources, out, notes, sems = refs[:owners], refs[owners], refs[owners + 1], refs[owners + 2]
    rows = ROW_TILES * TILE
    reads = [
        pltpu.make_async_copy(sources[n].at[pl.ds(rows, NOTE), pl.ds(0, 128)], notes.at[n], sems.at[PLANE * owners + n])
        for n in range(owners)
    ]
    for copy in reads:
        copy.start()
    copies = []
    for n in range(owners):
        reads[n].wait()
        for dest in range(PLANE):
            tile = jnp.clip(notes[n, 0, base[0] + dest].astype(jnp.int32), 0, ROW_TILES - 1)
            copy = pltpu.make_async_copy(
                sources[n].at[pl.ds(pl.multiple_of(tile * TILE, TILE), TILE)], out.at[dest, n], sems.at[n * PLANE + dest]
            )
            copy.start()
            copies.append(copy)
    for copy in copies:
        copy.wait()


def select(base, sources, micros):
    owners, cols = len(sources), sources[0].shape[1]
    return pl.pallas_call(
        select_kernel,
        out_shape=jax.ShapeDtypeStruct((PLANE, owners, TILE, cols), jnp.float32),
        in_specs=[SCALARS] + [IN_HBM] * owners,
        out_specs=INSIDE,
        scratch_shapes=[pltpu.SMEM((owners, NOTE, 128), jnp.float32), pltpu.SemaphoreType.DMA(((PLANE + 1) * owners,))],
        cost_estimate=cost(micros),
    )(base, *in_hbm(*sources))


def prepare_kernel(spot, i0, i1, i2, i3, out_hi, out_lo, held, sems):
    per = ROW_TILES * TERM_SHARE
    g = pl.program_id(0)

    @pl.when(g == 0)
    def _():
        copies = [
            pltpu.make_async_copy(piece, held.at[pl.ds(n * per, per)], sems.at[n])
            for n, piece in enumerate((i0, i1, i2, i3))
        ]
        for copy in copies:
            copy.start()
        for copy in copies:
            copy.wait()

    low = lax.broadcasted_iota(jnp.int32, (TILE // 2, 2 * TILE), 1) < TILE
    for x in range(ROW_TILES):
        for pair in range(GROUP // 2):
            s = g * GROUP + 2 * pair
            first = held[spot[x, s]]
            second = held[spot[x, s + 1]]
            top = jnp.where(low, first, pltpu.roll(second, TILE, 1))
            bottom = jnp.where(low, pltpu.roll(first, TILE, 1), second)
            for half, value in enumerate((top, bottom)):
                hi, lo = split(value)
                rows = pl.ds(x * TILE + half * (TILE // 2), TILE // 2)
                cols = pl.ds(pair * 2 * TILE, 2 * TILE)
                out_hi[rows, cols] = hi
                out_lo[rows, cols] = lo


def prepare(spot, pieces):
    rows, width = ROW_TILES * TILE, GROUP * TILE
    shape = jax.ShapeDtypeStruct((rows, OWNERS * TILE), jnp.bfloat16)
    block = pl.BlockSpec((rows, width), lambda g: (0, g))
    return pl.pallas_call(
        prepare_kernel,
        grid=(OWNERS // GROUP,),
        out_shape=(shape, shape),
        in_specs=[SCALARS] + [IN_HBM] * 4,
        out_specs=(block, block),
        scratch_shapes=[
            pltpu.VMEM((4 * ROW_TILES * TERM_SHARE, TILE // 2, 2 * TILE), jnp.float32),
            pltpu.SemaphoreType.DMA((4,)),
        ],
        compiler_params=PARAMS,
    )(spot, *in_hbm(*pieces))


def product(left_hi, left_lo, right):
    hi, lo = split(right)
    total = jnp.dot(left_hi, lo, preferred_element_type=jnp.float32)
    total += jnp.dot(left_lo, hi, preferred_element_type=jnp.float32)
    return total + jnp.dot(left_hi, hi, preferred_element_type=jnp.float32)


def steps_kernel(count, half, *refs):
    tiles, lefts, outs = refs[:count], refs[count : 3 * count], refs[3 * count :]
    for which in range(2):
        total = None
        for n in range(count):
            left_hi, left_lo = lefts[2 * n], lefts[2 * n + 1]
            depth = left_hi.shape[1] // XH
            part = pl.ds(which * depth, depth)
            value = tiles[n][half[0] ^ which].reshape(depth, tiles[n].shape[-1])
            term = product(left_hi[:, part], left_lo[:, part], value)
            total = term if total is None else total + term
        outs[which][...] = total


def column_block(rows, depth, index):
    return pl.BlockSpec((rows, depth), lambda g: (0, index))


def full(x):
    return pl.BlockSpec(x.shape, lambda g: (0,) * x.ndim)


def steps(half, tiles, indices, left, micros):
    rows, cols = left[0].shape[0], tiles[0].shape[-1]
    tiles = in_hbm(*[t.reshape(XH, Y, *t.shape[1:]) for t in tiles])
    shape = jax.ShapeDtypeStruct((rows, cols), jnp.float32)
    blocks = [column_block(rows, PLANE * t.shape[2] * TILE, index) for t, index in zip(tiles, indices)]
    return pl.pallas_call(
        functools.partial(steps_kernel, len(tiles)),
        grid=(1,),
        out_shape=(shape, shape),
        in_specs=[SCALARS] + [full(t) for t in tiles] + [block for block in blocks for _ in range(2)],
        out_specs=(full(shape), full(shape)),
        compiler_params=PARAMS,
        cost_estimate=cost(micros),
    )(half, *tiles, *(left * len(tiles)))


def last_kernel(tiles, left_hi, left_lo, total, other, amp, row_gap, col_gap, res, new):
    values = tiles[...].reshape(left_hi.shape[1], tiles.shape[-1])
    cycle = (total[...] + other[...] + product(left_hi[...], left_lo[...], values)).T
    column = jnp.broadcast_to(col_gap[...], (8, col_gap.shape[1])).T[:, :1]
    gap = column + row_gap[...]
    amplitudes = amp[...]
    residual = cycle - gap * amplitudes
    res[...] = residual
    new[...] = amplitudes + residual / gap


def last(offset, tiles, left, total, other, amp, row_gap, col_gap):
    rows, cols = left[0].shape[0], tiles.shape[-1]
    depth = PLANE * tiles.shape[1] * TILE
    (tiles,) = in_hbm(tiles)
    shape = jax.ShapeDtypeStruct((cols, rows), jnp.float32)
    block = pl.BlockSpec((pl.Element(rows), pl.Element(depth)), lambda g: (0, offset))
    return pl.pallas_call(
        last_kernel,
        grid=(1,),
        out_shape=(shape, shape),
        in_specs=[full(tiles), block, block, full(total), full(other), full(amp), full(row_gap), full(col_gap)],
        out_specs=(full(shape), full(shape)),
        compiler_params=PARAMS,
    )(tiles, *left, total, other, amp, row_gap, col_gap)


def tie_kernel(*refs):
    del refs


def tie(xs, after):
    return pl.pallas_call(
        tie_kernel,
        out_shape=[jax.ShapeDtypeStruct(x.shape, x.dtype) for x in xs],
        in_specs=[IN_HBM] * (len(xs) + len(after)),
        out_specs=[IN_HBM] * len(xs),
        input_output_aliases={n: n for n in range(len(xs))},
    )(*in_hbm(*xs, *after))


def pack_kernel(integrals, after, out):
    del after
    value = integrals[0]
    out[...] = jnp.concatenate([value[:, : TILE // 2], value[:, TILE // 2 :]], axis=2)


def pack(integrals, after):
    shape = (TERM_SHARE, TILE // 2, 2 * TILE)
    return pl.pallas_call(
        pack_kernel,
        grid=(ROW_TILES,),
        out_shape=jax.ShapeDtypeStruct((ROW_TILES * TERM_SHARE,) + shape[1:], jnp.float32),
        in_specs=[pl.BlockSpec((1,) + integrals.shape[1:], lambda x: (x, 0, 0, 0)), IN_HBM],
        out_specs=pl.BlockSpec(shape, lambda x: (x, 0, 0)),
    )(integrals, *in_hbm(after))


def swap(x, axis):
    return lax.ppermute(x, axis, [(0, 1), (1, 0)])


def shift(x, by):
    turns = [((z * CO + c), ((z + (by if c == 0 else -by)) % Z) * CO + c) for z in range(Z) for c in range(CO)]
    return lax.ppermute(x, ("z", "co"), turns)


def exchange(x, mirrored):
    if not mirrored:
        return lax.all_to_all(x, ("xh", "y"), 0, 0, tiled=True)
    groups = [[(xh * Y + y) * XL + (xh ^ d) for xh in range(XH) for y in range(Y)] for d in range(XL)]
    return lax.all_to_all(x, ("xh", "y", "xl"), 0, 0, axis_index_groups=groups, tiled=True)


def body(amplitudes, integrals, send_tiles, task_slots, row_gap, column_gap):
    z, half = lax.axis_index("z"), lax.axis_index("xh")
    core = lax.axis_index("co")
    sign = 1 - 2 * core
    base, half = (z * PLANE)[None].astype(jnp.int32), half[None].astype(jnp.int32)

    owned = first(amplitudes, send_tiles)
    packed = pack(integrals, owned)
    across = swap(packed, "xl")
    beside = swap(packed, "co")
    diagonal = swap(across, "co")

    ring = {0: owned}
    order, received = [], []
    for n, (offsets, mirrored) in enumerate(zip(STEPS, MIRRORED)):
        if n == len(STEPS) - 1:
            ring[n], ring[-n] = shift(ring[n - 1], 1), shift(ring[1 - n], -1)
            ring[n], ring[-n] = tie([ring[n], ring[-n]], [received[n - 2]])
            ring[n + 1] = shift(ring[n], 1)
        elif n > 0:
            ring[n], ring[-n] = shift(ring[n - 1], 1), shift(ring[1 - n], -1)
            if n > 1:
                ring[n], ring[-n] = tie([ring[n], ring[-n]], [received[n - 2]])
        outgoing = select(base, [ring[o] for o in offsets], SELECT_COST)
        received.append(exchange(outgoing, mirrored))
        places = (z - sign * jnp.array(offsets, jnp.int32)) % Z
        turn = half[0] if mirrored else 0
        peers = jnp.arange(PLANE, dtype=jnp.int32) ^ (turn * Y)
        order.append((places[None, :] * PLANE + peers[:, None]).reshape(-1))
    order = jnp.concatenate([order[n] for n in (1, 2, 0, 3)])

    mine = lax.axis_index("xl") * CO + core
    terms = jnp.arange(OWNERS, dtype=jnp.int32)
    term = jnp.sum(jnp.where(task_slots[:, None, :] == order[None, :, None], terms[None, None, :], 0), axis=2)
    relative = (term // TERM_SHARE) ^ mine
    spot = (relative * ROW_TILES + jnp.arange(ROW_TILES, dtype=jnp.int32)[:, None]) * TERM_SHARE + term % TERM_SHARE
    left = in_hbm(*prepare(spot, (packed, beside, across, diagonal)))

    total, other = steps(half, received[:3], (4, 0, 1), left, 60)
    other = swap(other, "xl")
    return last(5 * 512, received[3], left, total, other, amplitudes, row_gap[None, :], column_gap[None, :])


def solution(mesh):
    fine = Mesh(mesh.devices.reshape(Z, XH, Y, XL, CO), ("z", "xh", "y", "xl", "co"))
    wide, narrow = ("z", "xh", "y"), ("xl", "co")
    return jax.shard_map(
        body,
        mesh=fine,
        in_specs=(P(narrow, wide), P(wide, narrow, None, None), P(wide, None), P(wide, None), P(wide), P(narrow)),
        out_specs=(P(narrow, wide), P(narrow, wide)),
        check_vma=False,
    )
```

```python
import functools

import jax
import jax.numpy as jnp
from jax import lax
from jax.experimental import pallas as pl
from jax.experimental.pallas import tpu as pltpu
from jax.sharding import Mesh, PartitionSpec as P

Z, XH, Y, XL, CO = 8, 2, 4, 2, 2
PLANE = XH * Y
OWNERS = Z * PLANE
TILE = 64
ROW_TILES = 8
TERM_SHARE = 16
GROUP = 4
NOTE = 8
SELECT_COST = (40, 40, 40, 8, 30)
STEPS = ((0,), (1, -1), (2, -2), (3, -3), (4,))
MIRRORED = (True, True, True, False, False)
ANYWHERE = pl.BlockSpec(memory_space=pl.ANY)
IN_HBM = pl.BlockSpec(memory_space=pltpu.HBM)
INSIDE = pl.BlockSpec(memory_space=pltpu.VMEM)
SCALARS = pl.BlockSpec(memory_space=pltpu.SMEM)
PARAMS = pltpu.CompilerParams(vmem_limit_bytes=40 * 1024 * 1024)


def cost(micros):
    return pl.CostEstimate(flops=int(micros * 1e9), bytes_accessed=0, transcendentals=0)


def in_hbm(*xs):
    return [pltpu.with_memory_space_constraint(x, pltpu.HBM) for x in xs]


def split(x):
    hi = x.astype(jnp.bfloat16)
    lo = (x - hi.astype(jnp.float32)).astype(jnp.bfloat16)
    return hi, lo


def first_kernel(amp, send, out, held, sem):
    rows = amp.shape[1]
    held[pl.ds(0, rows)] = amp[...].T
    wide = jnp.pad(send[...].astype(jnp.float32), ((0, 0), (0, amp.shape[0] - OWNERS)))
    held[pl.ds(rows, NOTE)] = jnp.broadcast_to(wide, (NOTE, amp.shape[0]))
    copy = pltpu.make_async_copy(held, out, sem)
    copy.start()
    copy.wait()


def first(amp, send):
    cols, rows = amp.shape
    return pl.pallas_call(
        first_kernel,
        out_shape=jax.ShapeDtypeStruct((rows + NOTE, cols), jnp.float32),
        in_specs=[INSIDE, INSIDE],
        out_specs=IN_HBM,
        scratch_shapes=[pltpu.VMEM((rows + NOTE, cols), jnp.float32), pltpu.SemaphoreType.DMA],
    )(amp, send)


def select_kernel(base, *refs):
    owners = (len(refs) - 3)
    sources, out, notes, sems = refs[:owners], refs[owners], refs[owners + 1], refs[owners + 2]
    rows = ROW_TILES * TILE
    reads = [
        pltpu.make_async_copy(sources[n].at[pl.ds(rows, NOTE), pl.ds(0, 128)], notes.at[n], sems.at[PLANE * owners + n])
        for n in range(owners)
    ]
    for copy in reads:
        copy.start()
    copies = []
    for n in range(owners):
        reads[n].wait()
        for dest in range(PLANE):
            tile = jnp.clip(notes[n, 0, base[0] + dest].astype(jnp.int32), 0, ROW_TILES - 1)
            copy = pltpu.make_async_copy(
                sources[n].at[pl.ds(pl.multiple_of(tile * TILE, TILE), TILE)], out.at[dest, n], sems.at[n * PLANE + dest]
            )
            copy.start()
            copies.append(copy)
    for copy in copies:
        copy.wait()


def select(base, sources, micros):
    owners, cols = len(sources), sources[0].shape[1]
    return pl.pallas_call(
        select_kernel,
        out_shape=jax.ShapeDtypeStruct((PLANE, owners, TILE, cols), jnp.float32),
        in_specs=[SCALARS] + [IN_HBM] * owners,
        out_specs=INSIDE,
        scratch_shapes=[pltpu.SMEM((owners, NOTE, 128), jnp.float32), pltpu.SemaphoreType.DMA(((PLANE + 1) * owners,))],
        cost_estimate=cost(micros),
    )(base, *in_hbm(*sources))


def prepare_kernel(spot, i0, i1, i2, i3, out_hi, out_lo, held, sems):
    per = ROW_TILES * TERM_SHARE
    g = pl.program_id(0)

    @pl.when(g == 0)
    def _():
        copies = [
            pltpu.make_async_copy(piece, held.at[pl.ds(n * per, per)], sems.at[n])
            for n, piece in enumerate((i0, i1, i2, i3))
        ]
        for copy in copies:
            copy.start()
        for copy in copies:
            copy.wait()

    low = lax.broadcasted_iota(jnp.int32, (TILE // 2, 2 * TILE), 1) < TILE
    for x in range(ROW_TILES):
        for pair in range(GROUP // 2):
            s = g * GROUP + 2 * pair
            first = held[spot[x, s]]
            second = held[spot[x, s + 1]]
            top = jnp.where(low, first, pltpu.roll(second, TILE, 1))
            bottom = jnp.where(low, pltpu.roll(first, TILE, 1), second)
            for half, value in enumerate((top, bottom)):
                hi, lo = split(value)
                rows = pl.ds(x * TILE + half * (TILE // 2), TILE // 2)
                cols = pl.ds(pair * 2 * TILE, 2 * TILE)
                out_hi[rows, cols] = hi
                out_lo[rows, cols] = lo


def prepare(spot, pieces):
    rows, width = ROW_TILES * TILE, GROUP * TILE
    shape = jax.ShapeDtypeStruct((rows, OWNERS * TILE), jnp.bfloat16)
    block = pl.BlockSpec((rows, width), lambda g: (0, g))
    return pl.pallas_call(
        prepare_kernel,
        grid=(OWNERS // GROUP,),
        out_shape=(shape, shape),
        in_specs=[SCALARS] + [IN_HBM] * 4,
        out_specs=(block, block),
        scratch_shapes=[
            pltpu.VMEM((4 * ROW_TILES * TERM_SHARE, TILE // 2, 2 * TILE), jnp.float32),
            pltpu.SemaphoreType.DMA((4,)),
        ],
        compiler_params=PARAMS,
    )(spot, *in_hbm(*pieces))


def product(left_hi, left_lo, right):
    hi, lo = split(right)
    total = jnp.dot(left_hi, lo, preferred_element_type=jnp.float32)
    total += jnp.dot(left_lo, hi, preferred_element_type=jnp.float32)
    return total + jnp.dot(left_hi, hi, preferred_element_type=jnp.float32)


def steps_kernel(count, half, *refs):
    tiles, lefts, outs = refs[:count], refs[count : 3 * count], refs[3 * count :]
    for which in range(2):
        total = None
        for n in range(count):
            left_hi, left_lo = lefts[2 * n], lefts[2 * n + 1]
            depth = left_hi.shape[1] // XH
            part = pl.ds(which * depth, depth)
            value = tiles[n][half[0] ^ which].reshape(depth, tiles[n].shape[-1])
            term = product(left_hi[:, part], left_lo[:, part], value)
            total = term if total is None else total + term
        outs[which][...] = total


def column_block(rows, depth, index):
    return pl.BlockSpec((rows, depth), lambda g: (0, index))


def full(x):
    return pl.BlockSpec(x.shape, lambda g: (0,) * x.ndim)


def steps(half, tiles, indices, left, micros):
    rows, cols = left[0].shape[0], tiles[0].shape[-1]
    tiles = [t.reshape(XH, Y, *t.shape[1:]) for t in tiles]
    shape = jax.ShapeDtypeStruct((rows, cols), jnp.float32)
    blocks = [column_block(rows, PLANE * t.shape[2] * TILE, index) for t, index in zip(tiles, indices)]
    return pl.pallas_call(
        functools.partial(steps_kernel, len(tiles)),
        grid=(1,),
        out_shape=(shape, shape),
        in_specs=[SCALARS] + [full(t) for t in tiles] + [block for block in blocks for _ in range(2)],
        out_specs=(full(shape), full(shape)),
        compiler_params=PARAMS,
        cost_estimate=cost(micros),
    )(half, *tiles, *(left * len(tiles)))


def last_kernel(tiles, left_hi, left_lo, total, other, amp, row_gap, col_gap, res, new):
    values = tiles[...].reshape(left_hi.shape[1], tiles.shape[-1])
    cycle = (total[...] + other[...] + product(left_hi[...], left_lo[...], values)).T
    column = jnp.broadcast_to(col_gap[...], (8, col_gap.shape[1])).T[:, :1]
    gap = column + row_gap[...]
    amplitudes = amp[...]
    residual = cycle - gap * amplitudes
    res[...] = residual
    new[...] = amplitudes + residual / gap


def last(index, tiles, left, total, other, amp, row_gap, col_gap):
    rows, cols = left[0].shape[0], tiles.shape[-1]
    block = column_block(rows, PLANE * tiles.shape[1] * TILE, index)
    shape = jax.ShapeDtypeStruct((cols, rows), jnp.float32)
    return pl.pallas_call(
        last_kernel,
        grid=(1,),
        out_shape=(shape, shape),
        in_specs=[full(tiles), block, block, full(total), full(other), full(amp), full(row_gap), full(col_gap)],
        out_specs=(full(shape), full(shape)),
        compiler_params=PARAMS,
    )(tiles, *left, total, other, amp, row_gap, col_gap)


def more_kernel(tiles, left_hi, left_lo, total, out):
    values = tiles[...].reshape(left_hi.shape[1], tiles.shape[-1])
    out[...] = total[...] + product(left_hi[...], left_lo[...], values)


def more(index, tiles, left, total, micros):
    rows = left[0].shape[0]
    block = column_block(rows, PLANE * tiles.shape[1] * TILE, index)
    return pl.pallas_call(
        more_kernel,
        grid=(1,),
        out_shape=jax.ShapeDtypeStruct(total.shape, jnp.float32),
        in_specs=[full(tiles), block, block, full(total)],
        out_specs=full(total),
        compiler_params=PARAMS,
        cost_estimate=cost(micros),
    )(tiles, *left, total)


def tie_kernel(*refs):
    del refs


def tie(xs, after):
    return pl.pallas_call(
        tie_kernel,
        out_shape=[jax.ShapeDtypeStruct(x.shape, x.dtype) for x in xs],
        in_specs=[IN_HBM] * len(xs) + [ANYWHERE] * len(after),
        out_specs=[IN_HBM] * len(xs),
        input_output_aliases={n: n for n in range(len(xs))},
    )(*in_hbm(*xs), *after)


def pack_kernel(integrals, after, out):
    del after
    value = integrals[0]
    out[...] = jnp.concatenate([value[:, : TILE // 2], value[:, TILE // 2 :]], axis=2)


def pack(integrals, after):
    shape = (TERM_SHARE, TILE // 2, 2 * TILE)
    return pl.pallas_call(
        pack_kernel,
        grid=(ROW_TILES,),
        out_shape=jax.ShapeDtypeStruct((ROW_TILES * TERM_SHARE,) + shape[1:], jnp.float32),
        in_specs=[pl.BlockSpec((1,) + integrals.shape[1:], lambda x: (x, 0, 0, 0)), IN_HBM],
        out_specs=pl.BlockSpec(shape, lambda x: (x, 0, 0)),
    )(integrals, *in_hbm(after))


def swap(x, axis):
    return lax.ppermute(x, axis, [(0, 1), (1, 0)])


def shift(x, by):
    turns = [((z * CO + c), ((z + (by if c == 0 else -by)) % Z) * CO + c) for z in range(Z) for c in range(CO)]
    return lax.ppermute(x, ("z", "co"), turns)


def exchange(x, mirrored):
    if not mirrored:
        return lax.all_to_all(x, ("xh", "y"), 0, 0, tiled=True)
    groups = [[(xh * Y + y) * XL + (xh ^ d) for xh in range(XH) for y in range(Y)] for d in range(XL)]
    return lax.all_to_all(x, ("xh", "y", "xl"), 0, 0, axis_index_groups=groups, tiled=True)


def body(amplitudes, integrals, send_tiles, task_slots, row_gap, column_gap):
    z, half = lax.axis_index("z"), lax.axis_index("xh")
    core = lax.axis_index("co")
    sign = 1 - 2 * core
    base, half = (z * PLANE)[None].astype(jnp.int32), half[None].astype(jnp.int32)

    owned = first(amplitudes, send_tiles)
    ring = {0: owned}
    order, received = [], []
    for n, (offsets, mirrored) in enumerate(zip(STEPS, MIRRORED)):
        if n == Z // 2:
            ring[n] = shift(ring[n - 1], 1)
        elif n > 0:
            ring[n], ring[-n] = shift(ring[n - 1], 1), shift(ring[1 - n], -1)
            if n > 1:
                ring[n], ring[-n] = tie([ring[n], ring[-n]], [received[n - 2]])
        outgoing = select(base, [ring[o] for o in offsets], SELECT_COST[n])
        if n == 0:
            packed = pack(integrals, outgoing)
        received.append(exchange(outgoing, mirrored))
        places = (z - sign * jnp.array(offsets, jnp.int32)) % Z
        turn = half[0] if mirrored else 0
        peers = jnp.arange(PLANE, dtype=jnp.int32) ^ (turn * Y)
        order.append((places[None, :] * PLANE + peers[:, None]).reshape(-1))
    across = swap(packed, "xl")
    beside = swap(packed, "co")
    diagonal = swap(tie([across], [ring[3]])[0], "co")

    order = jnp.concatenate([order[n] for n in (1, 2, 3, 0, 4)])

    mine = lax.axis_index("xl") * CO + core
    terms = jnp.arange(OWNERS, dtype=jnp.int32)
    term = jnp.sum(jnp.where(task_slots[:, None, :] == order[None, :, None], terms[None, None, :], 0), axis=2)
    relative = (term // TERM_SHARE) ^ mine
    spot = (relative * ROW_TILES + jnp.arange(ROW_TILES, dtype=jnp.int32)[:, None]) * TERM_SHARE + term % TERM_SHARE
    left = in_hbm(*prepare(spot, (packed, beside, across, diagonal)))

    total, other = steps(half, received[:3], (6, 0, 1), left, 8)
    other = swap(other, "xl")
    total = more(2, received[3], left, total, 60)
    return last(7, received[4], left, total, other, amplitudes, row_gap[None, :], column_gap[None, :])


def solution(mesh):
    fine = Mesh(mesh.devices.reshape(Z, XH, Y, XL, CO), ("z", "xh", "y", "xl", "co"))
    wide, narrow = ("z", "xh", "y"), ("xl", "co")
    return jax.shard_map(
        body,
        mesh=fine,
        in_specs=(P(narrow, wide), P(wide, narrow, None, None), P(wide, None), P(wide, None), P(wide), P(narrow)),
        out_specs=(P(narrow, wide), P(narrow, wide)),
        check_vma=False,
    )
```

```python
import functools

import jax
import jax.numpy as jnp
from jax import lax
from jax.experimental import pallas as pl
from jax.experimental.pallas import tpu as pltpu
from jax.sharding import Mesh, PartitionSpec as P

Z, XH, Y, XL, CO = 8, 2, 4, 2, 2
PLANE = XH * Y
OWNERS = Z * PLANE
TILE = 64
ROW_TILES = 8
TERM_SHARE = 16
GROUP = 4
NOTE = 8
SELECT_COST = (3, 40, 40, 15, 30)
MORE_COST = 60
PACK_COST = 40
PREPARE_COST = 10
OTHER_COST = 3
OWN_COST = 60
STEPS = ((0,), (1, -1), (2, -2), (3, -3), (4,))
MIRRORED = (True, True, False, False, False)
ANYWHERE = pl.BlockSpec(memory_space=pl.ANY)
IN_HBM = pl.BlockSpec(memory_space=pltpu.HBM)
INSIDE = pl.BlockSpec(memory_space=pltpu.VMEM)
SCALARS = pl.BlockSpec(memory_space=pltpu.SMEM)
PARAMS = pltpu.CompilerParams(vmem_limit_bytes=65500 * 1024)


def cost(micros):
    return pl.CostEstimate(flops=int(micros * 1e9), bytes_accessed=0, transcendentals=0)


def in_hbm(*xs):
    return [pltpu.with_memory_space_constraint(x, pltpu.HBM) for x in xs]


def split(x):
    hi = x.astype(jnp.bfloat16)
    lo = (x - hi.astype(jnp.float32)).astype(jnp.bfloat16)
    return hi, lo


def first_kernel(amp, send, out, held, sem):
    rows = amp.shape[1]
    held[pl.ds(0, rows)] = amp[...].T
    wide = jnp.pad(send[...].astype(jnp.float32), ((0, 0), (0, amp.shape[0] - OWNERS)))
    held[pl.ds(rows, NOTE)] = jnp.broadcast_to(wide, (NOTE, amp.shape[0]))
    copy = pltpu.make_async_copy(held, out, sem)
    copy.start()
    copy.wait()


def first(amp, send):
    cols, rows = amp.shape
    return pl.pallas_call(
        first_kernel,
        compiler_params=PARAMS,
        out_shape=jax.ShapeDtypeStruct((rows + NOTE, cols), jnp.float32),
        in_specs=[INSIDE, INSIDE],
        out_specs=IN_HBM,
        scratch_shapes=[pltpu.VMEM((rows + NOTE, cols), jnp.float32), pltpu.SemaphoreType.DMA],
    )(amp, send)


def select_kernel(owners, base, *refs):
    sources, (out, notes, sems) = refs[:owners], refs[-3:]
    rows = ROW_TILES * TILE
    reads = [
        pltpu.make_async_copy(sources[n].at[pl.ds(rows, NOTE), pl.ds(0, 128)], notes.at[n], sems.at[PLANE * owners + n])
        for n in range(owners)
    ]
    for copy in reads:
        copy.start()
    copies = []
    for n in range(owners):
        reads[n].wait()
        for dest in range(PLANE):
            tile = jnp.clip(notes[n, 0, base[0] + dest].astype(jnp.int32), 0, ROW_TILES - 1)
            copy = pltpu.make_async_copy(
                sources[n].at[pl.ds(pl.multiple_of(tile * TILE, TILE), TILE)], out.at[dest, n], sems.at[n * PLANE + dest]
            )
            copy.start()
            copies.append(copy)
    for copy in copies:
        copy.wait()


def select(base, sources, after, micros):
    owners, cols = len(sources), sources[0].shape[1]
    return pl.pallas_call(
        functools.partial(select_kernel, owners),
        compiler_params=PARAMS,
        out_shape=jax.ShapeDtypeStruct((PLANE, owners, TILE, cols), jnp.float32),
        in_specs=[SCALARS] + [IN_HBM] * owners + [ANYWHERE] * len(after),
        out_specs=INSIDE,
        scratch_shapes=[pltpu.SMEM((owners, NOTE, 128), jnp.float32), pltpu.SemaphoreType.DMA(((PLANE + 1) * owners,))],
        cost_estimate=cost(micros),
    )(base, *in_hbm(*sources), *after)


def prepare_kernel(spot, i0, i1, i2, i3, out_hi, out_lo, held, stage_hi, stage_lo, sems, out_sems):
    per = ROW_TILES * TERM_SHARE
    g, groups = pl.program_id(0), OWNERS // GROUP
    slot, width = g % 2, GROUP * TILE

    @pl.when(g == 0)
    def _():
        copies = [
            pltpu.make_async_copy(piece, held.at[pl.ds(n * per, per)], sems.at[n])
            for n, piece in enumerate((i0, i1, i2, i3))
        ]
        for copy in copies:
            copy.start()
        for copy in copies:
            copy.wait()

    def leave(step):
        cols = pl.ds(pl.multiple_of(step * width, width), width)
        return [
            pltpu.make_async_copy(stage.at[step % 2], out.at[:, cols], out_sems.at[n, step % 2])
            for n, (stage, out) in enumerate(((stage_hi, out_hi), (stage_lo, out_lo)))
        ]

    @pl.when(g >= 2)
    def _():
        for copy in leave(g - 2):
            copy.wait()

    low = lax.broadcasted_iota(jnp.int32, (TILE // 2, 2 * TILE), 1) < TILE
    for x in range(ROW_TILES):
        for pair in range(GROUP // 2):
            s = g * GROUP + 2 * pair
            first = held[spot[x, s]]
            second = held[spot[x, s + 1]]
            top = jnp.where(low, first, pltpu.roll(second, TILE, 1))
            bottom = jnp.where(low, pltpu.roll(first, TILE, 1), second)
            for half, value in enumerate((top, bottom)):
                hi, lo = split(value)
                rows = pl.ds(x * TILE + half * (TILE // 2), TILE // 2)
                cols = pl.ds(pair * 2 * TILE, 2 * TILE)
                stage_hi[slot, rows, cols] = hi
                stage_lo[slot, rows, cols] = lo
    for copy in leave(g):
        copy.start()

    @pl.when(g == groups - 1)
    def _():
        for copy in leave(g - 1) + leave(g):
            copy.wait()


def prepare(spot, pieces):
    rows, width = ROW_TILES * TILE, GROUP * TILE
    shape = jax.ShapeDtypeStruct((rows, OWNERS * TILE), jnp.bfloat16)
    return pl.pallas_call(
        prepare_kernel,
        grid=(OWNERS // GROUP,),
        out_shape=(shape, shape),
        in_specs=[SCALARS] + [ANYWHERE] * 4,
        out_specs=(IN_HBM, IN_HBM),
        scratch_shapes=[
            pltpu.VMEM((4 * ROW_TILES * TERM_SHARE, TILE // 2, 2 * TILE), jnp.float32),
            pltpu.VMEM((2, rows, width), jnp.bfloat16),
            pltpu.VMEM((2, rows, width), jnp.bfloat16),
            pltpu.SemaphoreType.DMA((4,)),
            pltpu.SemaphoreType.DMA((2, 2)),
        ],
        compiler_params=PARAMS,
        cost_estimate=cost(PREPARE_COST),
    )(spot, *pieces)


def product(left_hi, left_lo, right):
    hi, lo = split(right)
    total = jnp.dot(left_hi, lo, preferred_element_type=jnp.float32)
    total += jnp.dot(left_lo, hi, preferred_element_type=jnp.float32)
    return total + jnp.dot(left_hi, hi, preferred_element_type=jnp.float32)


def steps_kernel(parts, half, *refs):
    count = len(parts)
    tiles, lefts, out = refs[:count], refs[count : 3 * count], refs[3 * count]
    total = None
    for n, part in enumerate(parts):
        value = tiles[n][...].reshape(-1, tiles[n].shape[-1])
        term = product(lefts[2 * n][...], lefts[2 * n + 1][...], value)
        total = term if total is None else total + term
    out[...] = total


def full(x):
    return pl.BlockSpec(x.shape, lambda g: (0,) * x.ndim)


def steps(half, tiles, offsets, parts, left, micros):
    rows, cols = left[0].shape[0], tiles[0].shape[-1]
    shape = jax.ShapeDtypeStruct((rows, cols), jnp.float32)
    tile_specs, left_specs, lefts = [], [], []
    for t, offset, part in zip(tiles, offsets, parts):
        sources = PLANE if part is None else Y
        depth = sources * t.shape[1] * TILE
        block = (sources,) + t.shape[1:]
        if part is None:
            tile_specs.append(pl.BlockSpec(block, lambda g, half: (0, 0, 0, 0)))
            index = offset // depth
        else:
            tile_specs.append(pl.BlockSpec(block, functools.partial(lambda p, g, half: (half[0] ^ p, 0, 0, 0), part)))
            index = offset // depth + part
        left_specs += [pl.BlockSpec((rows, depth), functools.partial(lambda i, g, half: (0, i), index))] * 2
        lefts += left
    return pl.pallas_call(
        functools.partial(steps_kernel, parts),
        out_shape=shape,
        grid_spec=pltpu.PrefetchScalarGridSpec(
            num_scalar_prefetch=1,
            grid=(1,),
            in_specs=tile_specs + left_specs,
            out_specs=pl.BlockSpec((rows, cols), lambda g, half: (0, 0)),
        ),
        compiler_params=PARAMS,
        cost_estimate=cost(micros),
    )(half, *tiles, *lefts)


def last_kernel(tiles, left_hi, left_lo, total, other, amp, row_gap, col_gap, res, new):
    values = tiles[...].reshape(left_hi.shape[1], tiles.shape[-1])
    cycle = (total[...] + other[...] + product(left_hi[...], left_lo[...], values)).T
    column = jnp.broadcast_to(col_gap[...], (8, col_gap.shape[1])).T[:, :1]
    gap = column + row_gap[...]
    amplitudes = amp[...]
    residual = cycle - gap * amplitudes
    res[...] = residual
    new[...] = amplitudes + residual / gap


def last(offset, tiles, left, total, other, amp, row_gap, col_gap):
    rows, cols = left[0].shape[0], tiles.shape[-1]
    depth = PLANE * tiles.shape[1] * TILE
    block = pl.BlockSpec((pl.Element(rows), pl.Element(depth)), lambda g: (0, offset))
    shape = jax.ShapeDtypeStruct((cols, rows), jnp.float32)
    return pl.pallas_call(
        last_kernel,
        grid=(1,),
        out_shape=(shape, shape),
        in_specs=[full(tiles), block, block, full(total), full(other), full(amp), full(row_gap), full(col_gap)],
        out_specs=(full(shape), full(shape)),
        compiler_params=PARAMS,
    )(tiles, *left, total, other, amp, row_gap, col_gap)


def more_kernel(tiles, left_hi, left_lo, total, out):
    values = tiles[...].reshape(left_hi.shape[1], tiles.shape[-1])
    out[...] = total[...] + product(left_hi[...], left_lo[...], values)


def more(index, tiles, left, total, micros):
    rows = left[0].shape[0]
    block = pl.BlockSpec((rows, PLANE * tiles.shape[1] * TILE), lambda g: (0, index))
    return pl.pallas_call(
        more_kernel,
        grid=(1,),
        out_shape=jax.ShapeDtypeStruct(total.shape, jnp.float32),
        in_specs=[full(tiles), block, block, full(total)],
        out_specs=full(total),
        compiler_params=PARAMS,
        cost_estimate=cost(micros),
    )(tiles, *left, total)


def tie_kernel(*refs):
    del refs


def tie(xs, after):
    return pl.pallas_call(
        tie_kernel,
        compiler_params=PARAMS,
        out_shape=[jax.ShapeDtypeStruct(x.shape, x.dtype) for x in xs],
        in_specs=[IN_HBM] * len(xs) + [ANYWHERE] * len(after),
        out_specs=[IN_HBM] * len(xs),
        input_output_aliases={n: n for n in range(len(xs))},
    )(*in_hbm(*xs), *after)


def pack_kernel(integrals, after, out):
    del after
    value = integrals[0]
    out[...] = jnp.concatenate([value[:, : TILE // 2], value[:, TILE // 2 :]], axis=2)


def pack(integrals, after):
    shape = (TERM_SHARE, TILE // 2, 2 * TILE)
    return pl.pallas_call(
        pack_kernel,
        grid=(ROW_TILES,),
        compiler_params=PARAMS,
        out_shape=jax.ShapeDtypeStruct((ROW_TILES * TERM_SHARE,) + shape[1:], jnp.float32),
        in_specs=[pl.BlockSpec((1,) + integrals.shape[1:], lambda x: (x, 0, 0, 0)), IN_HBM],
        out_specs=pl.BlockSpec(shape, lambda x: (x, 0, 0)),
        cost_estimate=cost(PACK_COST),
    )(integrals, *in_hbm(after))


def swap(x, axis):
    return lax.ppermute(x, axis, [(0, 1), (1, 0)])


def shift(x, by):
    turns = [((z * CO + c), ((z + (by if c == 0 else -by)) % Z) * CO + c) for z in range(Z) for c in range(CO)]
    return lax.ppermute(x, ("z", "co"), turns)


def exchange(x, mirrored):
    if not mirrored:
        return lax.all_to_all(x, ("xh", "y"), 0, 0, tiled=True)
    groups = [[(xh * Y + y) * XL + (xh ^ d) for xh in range(XH) for y in range(Y)] for d in range(XL)]
    return lax.all_to_all(x, ("xh", "y", "xl"), 0, 0, axis_index_groups=groups, tiled=True)


def body(amplitudes, integrals, send_tiles, task_slots, row_gap, column_gap):
    z, half = lax.axis_index("z"), lax.axis_index("xh")
    core = lax.axis_index("co")
    sign = 1 - 2 * core
    base, half = (z * PLANE)[None].astype(jnp.int32), half[None].astype(jnp.int32)

    owned = first(amplitudes, send_tiles)
    packed = pack(integrals, owned)
    across = swap(packed, "xl")
    beside = swap(packed, "co")

    order = []
    for offsets, mirrored in zip(STEPS, MIRRORED):
        places = (z - sign * jnp.array(offsets, jnp.int32)) % Z
        turn = half[0] if mirrored else 0
        peers = jnp.arange(PLANE, dtype=jnp.int32) ^ (turn * Y)
        order.append((places[None, :] * PLANE + peers[:, None]).reshape(-1))
    order = jnp.concatenate([order[n] for n in (1, 2, 3, 0, 4)])
    mine = lax.axis_index("xl") * CO + core
    terms = jnp.arange(OWNERS, dtype=jnp.int32)
    term = jnp.sum(jnp.where(task_slots[:, None, :] == order[None, :, None], terms[None, None, :], 0), axis=2)
    relative = (term // TERM_SHARE) ^ mine
    spot = (relative * ROW_TILES + jnp.arange(ROW_TILES, dtype=jnp.int32)[:, None]) * TERM_SHARE + term % TERM_SHARE

    ring = {0: owned}
    received, left, other = [], [], None
    for n, (offsets, mirrored) in enumerate(zip(STEPS, MIRRORED)):
        if n == Z // 2:
            ring[n] = shift(ring[n - 1], 1)
        elif n > 0:
            ring[n], ring[-n] = shift(ring[n - 1], 1), shift(ring[1 - n], -1)
            if n > 1:
                ring[n], ring[-n] = tie([ring[n], ring[-n]], [received[n - 2]])
        if n == 3:
            left = in_hbm(*prepare(spot, (packed, beside, across, swap(across, "co"))))
        after = {0: [packed], 3: left[:1], 4: [other]}.get(n, [])
        outgoing = select(base, [ring[o] for o in offsets], after, SELECT_COST[n])
        received.append(exchange(outgoing, mirrored))
        if n == 3:
            other = steps(half, received[:2], (3072, 0), (1, 1), left, OTHER_COST)
    other = swap(other, "xl")
    total = steps(half, received[:3], (3072, 0, 1024), (0, 0, None), left, OWN_COST)
    total = more(2, received[3], left, total, MORE_COST)
    return last(3584, received[4], left, total, other, amplitudes, row_gap[None, :], column_gap[None, :])


def solution(mesh):
    fine = Mesh(mesh.devices.reshape(Z, XH, Y, XL, CO), ("z", "xh", "y", "xl", "co"))
    wide, narrow = ("z", "xh", "y"), ("xl", "co")
    return jax.shard_map(
        body,
        mesh=fine,
        in_specs=(P(narrow, wide), P(wide, narrow, None, None), P(wide, None), P(wide, None), P(wide), P(narrow)),
        out_specs=(P(narrow, wide), P(narrow, wide)),
        check_vma=False,
    )
```

```python
import functools

import jax
import jax.numpy as jnp
from jax import lax
from jax.experimental import pallas as pl
from jax.experimental.pallas import tpu as pltpu
from jax.sharding import Mesh, PartitionSpec as P

Z, XH, Y, XL, CO = 8, 2, 4, 2, 2
PLANE = XH * Y
OWNERS = Z * PLANE
TILE = 64
ROW_TILES = 8
TERM_SHARE = 16
GROUP = 4
NOTE = 8
SELECT_COST = (40, 40, 40, 15, 30)
MORE_COST = 60
PACK_COST = 40
PREPARE_COST = 3
OTHER_COST = 3
OWN_COST = 10
STEPS = ((0,), (1, -1), (2, -2), (3, -3), (4,))
MIRRORED = (True, True, True, False, False)
ANYWHERE = pl.BlockSpec(memory_space=pl.ANY)
IN_HBM = pl.BlockSpec(memory_space=pltpu.HBM)
INSIDE = pl.BlockSpec(memory_space=pltpu.VMEM)
SCALARS = pl.BlockSpec(memory_space=pltpu.SMEM)
PARAMS = pltpu.CompilerParams(vmem_limit_bytes=65500 * 1024)


def cost(micros):
    return pl.CostEstimate(flops=int(micros * 1e9), bytes_accessed=0, transcendentals=0)


def in_hbm(*xs):
    return [pltpu.with_memory_space_constraint(x, pltpu.HBM) for x in xs]


def split(x):
    hi = x.astype(jnp.bfloat16)
    lo = (x - hi.astype(jnp.float32)).astype(jnp.bfloat16)
    return hi, lo


def first_kernel(amp, send, out, held, sem):
    rows = amp.shape[1]
    held[pl.ds(0, rows)] = amp[...].T
    wide = jnp.pad(send[...].astype(jnp.float32), ((0, 0), (0, amp.shape[0] - OWNERS)))
    held[pl.ds(rows, NOTE)] = jnp.broadcast_to(wide, (NOTE, amp.shape[0]))
    copy = pltpu.make_async_copy(held, out, sem)
    copy.start()
    copy.wait()


def first(amp, send):
    cols, rows = amp.shape
    return pl.pallas_call(
        first_kernel,
        compiler_params=PARAMS,
        out_shape=jax.ShapeDtypeStruct((rows + NOTE, cols), jnp.float32),
        in_specs=[INSIDE, INSIDE],
        out_specs=IN_HBM,
        scratch_shapes=[pltpu.VMEM((rows + NOTE, cols), jnp.float32), pltpu.SemaphoreType.DMA],
    )(amp, send)


def select_kernel(base, *refs):
    owners = (len(refs) - 3)
    sources, out, notes, sems = refs[:owners], refs[owners], refs[owners + 1], refs[owners + 2]
    rows = ROW_TILES * TILE
    reads = [
        pltpu.make_async_copy(sources[n].at[pl.ds(rows, NOTE), pl.ds(0, 128)], notes.at[n], sems.at[PLANE * owners + n])
        for n in range(owners)
    ]
    for copy in reads:
        copy.start()
    copies = []
    for n in range(owners):
        reads[n].wait()
        for dest in range(PLANE):
            tile = jnp.clip(notes[n, 0, base[0] + dest].astype(jnp.int32), 0, ROW_TILES - 1)
            copy = pltpu.make_async_copy(
                sources[n].at[pl.ds(pl.multiple_of(tile * TILE, TILE), TILE)], out.at[dest, n], sems.at[n * PLANE + dest]
            )
            copy.start()
            copies.append(copy)
    for copy in copies:
        copy.wait()


def select(base, sources, micros):
    owners, cols = len(sources), sources[0].shape[1]
    return pl.pallas_call(
        select_kernel,
        compiler_params=PARAMS,
        out_shape=jax.ShapeDtypeStruct((PLANE, owners, TILE, cols), jnp.float32),
        in_specs=[SCALARS] + [IN_HBM] * owners,
        out_specs=INSIDE,
        scratch_shapes=[pltpu.SMEM((owners, NOTE, 128), jnp.float32), pltpu.SemaphoreType.DMA(((PLANE + 1) * owners,))],
        cost_estimate=cost(micros),
    )(base, *in_hbm(*sources))


def prepare_kernel(spot, i0, i1, i2, i3, out_hi, out_lo, held, sems):
    per = ROW_TILES * TERM_SHARE
    g = pl.program_id(0)

    @pl.when(g == 0)
    def _():
        copies = [
            pltpu.make_async_copy(piece, held.at[pl.ds(n * per, per)], sems.at[n])
            for n, piece in enumerate((i0, i1, i2, i3))
        ]
        for copy in copies:
            copy.start()
        for copy in copies:
            copy.wait()

    low = lax.broadcasted_iota(jnp.int32, (TILE // 2, 2 * TILE), 1) < TILE
    for x in range(ROW_TILES):
        for pair in range(GROUP // 2):
            s = g * GROUP + 2 * pair
            first = held[spot[x, s]]
            second = held[spot[x, s + 1]]
            top = jnp.where(low, first, pltpu.roll(second, TILE, 1))
            bottom = jnp.where(low, pltpu.roll(first, TILE, 1), second)
            for half, value in enumerate((top, bottom)):
                hi, lo = split(value)
                rows = pl.ds(x * TILE + half * (TILE // 2), TILE // 2)
                cols = pl.ds(pair * 2 * TILE, 2 * TILE)
                out_hi[rows, cols] = hi
                out_lo[rows, cols] = lo


def prepare(spot, pieces):
    rows, width = ROW_TILES * TILE, GROUP * TILE
    shape = jax.ShapeDtypeStruct((rows, OWNERS * TILE), jnp.bfloat16)
    block = pl.BlockSpec((rows, width), lambda g: (0, g))
    return pl.pallas_call(
        prepare_kernel,
        grid=(OWNERS // GROUP,),
        out_shape=(shape, shape),
        in_specs=[SCALARS] + [IN_HBM] * 4,
        out_specs=(block, block),
        scratch_shapes=[
            pltpu.VMEM((4 * ROW_TILES * TERM_SHARE, TILE // 2, 2 * TILE), jnp.float32),
            pltpu.SemaphoreType.DMA((4,)),
        ],
        compiler_params=PARAMS,
        cost_estimate=cost(PREPARE_COST),
    )(spot, *in_hbm(*pieces))


def product(left_hi, left_lo, right):
    hi, lo = split(right)
    total = jnp.dot(left_hi, lo, preferred_element_type=jnp.float32)
    total += jnp.dot(left_lo, hi, preferred_element_type=jnp.float32)
    return total + jnp.dot(left_hi, hi, preferred_element_type=jnp.float32)


def steps_kernel(parts, half, *refs):
    count = len(parts)
    tiles, lefts, out = refs[:count], refs[count : 3 * count], refs[3 * count]
    total = None
    for n, part in enumerate(parts):
        value = tiles[n][...].reshape(-1, tiles[n].shape[-1])
        term = product(lefts[2 * n][...], lefts[2 * n + 1][...], value)
        total = term if total is None else total + term
    out[...] = total


def full(x):
    return pl.BlockSpec(x.shape, lambda g: (0,) * x.ndim)


def steps(half, tiles, offsets, parts, left, micros):
    rows, cols = left[0].shape[0], tiles[0].shape[-1]
    shape = jax.ShapeDtypeStruct((rows, cols), jnp.float32)
    tile_specs, left_specs, lefts = [], [], []
    for t, offset, part in zip(tiles, offsets, parts):
        sources = PLANE if part is None else Y
        depth = sources * t.shape[1] * TILE
        block = (sources,) + t.shape[1:]
        if part is None:
            tile_specs.append(pl.BlockSpec(block, lambda g, half: (0, 0, 0, 0)))
            index = offset // depth
        else:
            tile_specs.append(pl.BlockSpec(block, functools.partial(lambda p, g, half: (half[0] ^ p, 0, 0, 0), part)))
            index = offset // depth + part
        left_specs += [pl.BlockSpec((rows, depth), functools.partial(lambda i, g, half: (0, i), index))] * 2
        lefts += left
    return pl.pallas_call(
        functools.partial(steps_kernel, parts),
        out_shape=shape,
        grid_spec=pltpu.PrefetchScalarGridSpec(
            num_scalar_prefetch=1,
            grid=(1,),
            in_specs=tile_specs + left_specs,
            out_specs=pl.BlockSpec((rows, cols), lambda g, half: (0, 0)),
        ),
        compiler_params=PARAMS,
        cost_estimate=cost(micros),
    )(half, *tiles, *lefts)


def last_kernel(tiles, left_hi, left_lo, total, other, amp, row_gap, col_gap, res, new):
    values = tiles[...].reshape(left_hi.shape[1], tiles.shape[-1])
    cycle = (total[...] + other[...] + product(left_hi[...], left_lo[...], values)).T
    column = jnp.broadcast_to(col_gap[...], (8, col_gap.shape[1])).T[:, :1]
    gap = column + row_gap[...]
    amplitudes = amp[...]
    residual = cycle - gap * amplitudes
    res[...] = residual
    new[...] = amplitudes + residual / gap


def last(offset, tiles, left, total, other, amp, row_gap, col_gap):
    rows, cols = left[0].shape[0], tiles.shape[-1]
    depth = PLANE * tiles.shape[1] * TILE
    block = pl.BlockSpec((pl.Element(rows), pl.Element(depth)), lambda g: (0, offset))
    shape = jax.ShapeDtypeStruct((cols, rows), jnp.float32)
    return pl.pallas_call(
        last_kernel,
        grid=(1,),
        out_shape=(shape, shape),
        in_specs=[full(tiles), block, block, full(total), full(other), full(amp), full(row_gap), full(col_gap)],
        out_specs=(full(shape), full(shape)),
        compiler_params=PARAMS,
    )(tiles, *left, total, other, amp, row_gap, col_gap)


def more_kernel(tiles, left_hi, left_lo, total, out):
    values = tiles[...].reshape(left_hi.shape[1], tiles.shape[-1])
    out[...] = total[...] + product(left_hi[...], left_lo[...], values)


def more(index, tiles, left, total, micros):
    rows = left[0].shape[0]
    block = pl.BlockSpec((rows, PLANE * tiles.shape[1] * TILE), lambda g: (0, index))
    return pl.pallas_call(
        more_kernel,
        grid=(1,),
        out_shape=jax.ShapeDtypeStruct(total.shape, jnp.float32),
        in_specs=[full(tiles), block, block, full(total)],
        out_specs=full(total),
        compiler_params=PARAMS,
        cost_estimate=cost(micros),
    )(tiles, *left, total)


def tie_kernel(*refs):
    del refs


def tie(xs, after):
    return pl.pallas_call(
        tie_kernel,
        compiler_params=PARAMS,
        out_shape=[jax.ShapeDtypeStruct(x.shape, x.dtype) for x in xs],
        in_specs=[IN_HBM] * len(xs) + [ANYWHERE] * len(after),
        out_specs=[IN_HBM] * len(xs),
        input_output_aliases={n: n for n in range(len(xs))},
    )(*in_hbm(*xs), *after)


def pack_kernel(integrals, after, out):
    del after
    value = integrals[0]
    out[...] = jnp.concatenate([value[:, : TILE // 2], value[:, TILE // 2 :]], axis=2)


def pack(integrals, after):
    shape = (TERM_SHARE, TILE // 2, 2 * TILE)
    return pl.pallas_call(
        pack_kernel,
        grid=(ROW_TILES,),
        compiler_params=PARAMS,
        out_shape=jax.ShapeDtypeStruct((ROW_TILES * TERM_SHARE,) + shape[1:], jnp.float32),
        in_specs=[pl.BlockSpec((1,) + integrals.shape[1:], lambda x: (x, 0, 0, 0)), IN_HBM],
        out_specs=pl.BlockSpec(shape, lambda x: (x, 0, 0)),
        cost_estimate=cost(PACK_COST),
    )(integrals, *in_hbm(after))


def swap(x, axis):
    return lax.ppermute(x, axis, [(0, 1), (1, 0)])


def shift(x, by):
    turns = [((z * CO + c), ((z + (by if c == 0 else -by)) % Z) * CO + c) for z in range(Z) for c in range(CO)]
    return lax.ppermute(x, ("z", "co"), turns)


def exchange(x, mirrored):
    if not mirrored:
        return lax.all_to_all(x, ("xh", "y"), 0, 0, tiled=True)
    groups = [[(xh * Y + y) * XL + (xh ^ d) for xh in range(XH) for y in range(Y)] for d in range(XL)]
    return lax.all_to_all(x, ("xh", "y", "xl"), 0, 0, axis_index_groups=groups, tiled=True)


def body(amplitudes, integrals, send_tiles, task_slots, row_gap, column_gap):
    z, half = lax.axis_index("z"), lax.axis_index("xh")
    core = lax.axis_index("co")
    sign = 1 - 2 * core
    base, half = (z * PLANE)[None].astype(jnp.int32), half[None].astype(jnp.int32)

    owned = first(amplitudes, send_tiles)
    ring = {0: owned}
    order, received = [], []
    for n, (offsets, mirrored) in enumerate(zip(STEPS, MIRRORED)):
        if n == Z // 2:
            ring[n] = shift(ring[n - 1], 1)
        elif n > 0:
            ring[n], ring[-n] = shift(ring[n - 1], 1), shift(ring[1 - n], -1)
            if n > 1:
                ring[n], ring[-n] = tie([ring[n], ring[-n]], [received[n - 2]])
        outgoing = select(base, [ring[o] for o in offsets], SELECT_COST[n])
        if n == 0:
            packed = pack(integrals, outgoing)
        received.append(exchange(outgoing, mirrored))
        places = (z - sign * jnp.array(offsets, jnp.int32)) % Z
        turn = half[0] if mirrored else 0
        peers = jnp.arange(PLANE, dtype=jnp.int32) ^ (turn * Y)
        order.append((places[None, :] * PLANE + peers[:, None]).reshape(-1))
    across = swap(packed, "xl")
    beside = swap(packed, "co")
    (across,) = tie([across], [ring[3]])
    diagonal = swap(across, "co")

    order = jnp.concatenate([order[n] for n in (1, 2, 3, 0, 4)])

    mine = lax.axis_index("xl") * CO + core
    terms = jnp.arange(OWNERS, dtype=jnp.int32)
    term = jnp.sum(jnp.where(task_slots[:, None, :] == order[None, :, None], terms[None, None, :], 0), axis=2)
    relative = (term // TERM_SHARE) ^ mine
    spot = (relative * ROW_TILES + jnp.arange(ROW_TILES, dtype=jnp.int32)[:, None]) * TERM_SHARE + term % TERM_SHARE
    left = in_hbm(*prepare(spot, (packed, beside, across, diagonal)))

    other = steps(half, received[:3], (3072, 0, 1024), (1, 1, 1), left, OTHER_COST)
    other = swap(other, "xl")
    total = steps(half, received[:3], (3072, 0, 1024), (0, 0, 0), left, OWN_COST)
    total = more(2, received[3], left, total, MORE_COST)
    return last(3584, received[4], left, total, other, amplitudes, row_gap[None, :], column_gap[None, :])


def solution(mesh):
    fine = Mesh(mesh.devices.reshape(Z, XH, Y, XL, CO), ("z", "xh", "y", "xl", "co"))
    wide, narrow = ("z", "xh", "y"), ("xl", "co")
    return jax.shard_map(
        body,
        mesh=fine,
        in_specs=(P(narrow, wide), P(wide, narrow, None, None), P(wide, None), P(wide, None), P(wide), P(narrow)),
        out_specs=(P(narrow, wide), P(narrow, wide)),
        check_vma=False,
    )
```

```python
import functools

import jax
import jax.numpy as jnp
from jax import lax
from jax.experimental import pallas as pl
from jax.experimental.pallas import tpu as pltpu
from jax.sharding import Mesh, PartitionSpec as P

Z, XH, Y, XL, CO = 8, 2, 4, 2, 2
PLANE = XH * Y
OWNERS = Z * PLANE
TILE = 64
ROW_TILES = 8
TERM_SHARE = 16
GROUP = 4
NOTE = 8
SELECT_COST = (3, 40, 40, 15)
PREPARE_COSTS = (10, 10)
MORE_COST = 60
PACK_COST = 40
PREPARE_COST = 10
OTHER_COST = 3
OWN_COST = 60
STEPS = ((0,), (1, -1), (2, -2), (3, -3, 4))
MIRRORED = (True, True, True, False)
ANYWHERE = pl.BlockSpec(memory_space=pl.ANY)
IN_HBM = pl.BlockSpec(memory_space=pltpu.HBM)
INSIDE = pl.BlockSpec(memory_space=pltpu.VMEM)
SCALARS = pl.BlockSpec(memory_space=pltpu.SMEM)
PARAMS = pltpu.CompilerParams(vmem_limit_bytes=65500 * 1024)


def cost(micros):
    return pl.CostEstimate(flops=int(micros * 1e9), bytes_accessed=0, transcendentals=0)


def in_hbm(*xs):
    return [pltpu.with_memory_space_constraint(x, pltpu.HBM) for x in xs]


def split(x):
    hi = x.astype(jnp.bfloat16)
    lo = (x - hi.astype(jnp.float32)).astype(jnp.bfloat16)
    return hi, lo


def first_kernel(amp, send, out, held, sem):
    rows = amp.shape[1]
    held[pl.ds(0, rows)] = amp[...].T
    wide = jnp.pad(send[...].astype(jnp.float32), ((0, 0), (0, amp.shape[0] - OWNERS)))
    held[pl.ds(rows, NOTE)] = jnp.broadcast_to(wide, (NOTE, amp.shape[0]))
    copy = pltpu.make_async_copy(held, out, sem)
    copy.start()
    copy.wait()


def first(amp, send):
    cols, rows = amp.shape
    return pl.pallas_call(
        first_kernel,
        compiler_params=PARAMS,
        out_shape=jax.ShapeDtypeStruct((rows + NOTE, cols), jnp.float32),
        in_specs=[INSIDE, INSIDE],
        out_specs=IN_HBM,
        scratch_shapes=[pltpu.VMEM((rows + NOTE, cols), jnp.float32), pltpu.SemaphoreType.DMA],
    )(amp, send)


def select_kernel(owners, meta, *refs):
    sources, (out, notes, sems) = refs[:owners], refs[-3:]
    rows = ROW_TILES * TILE
    reads = [
        pltpu.make_async_copy(sources[n].at[pl.ds(rows, NOTE), pl.ds(0, 128)], notes.at[n], sems.at[PLANE * owners + n])
        for n in range(owners)
    ]
    for copy in reads:
        copy.start()
    copies = []
    for n in range(owners):
        reads[n].wait()
        for dest in range(PLANE):
            tile = jnp.clip(notes[n, 0, meta[0] * PLANE + dest].astype(jnp.int32), 0, ROW_TILES - 1)
            copy = pltpu.make_async_copy(
                sources[n].at[pl.ds(pl.multiple_of(tile * TILE, TILE), TILE)], out.at[dest, n], sems.at[n * PLANE + dest]
            )
            copy.start()
            copies.append(copy)
    for copy in copies:
        copy.wait()


def select(meta, sources, after, micros):
    owners, cols = len(sources), sources[0].shape[1]
    return pl.pallas_call(
        functools.partial(select_kernel, owners),
        compiler_params=PARAMS,
        out_shape=jax.ShapeDtypeStruct((PLANE, owners, TILE, cols), jnp.float32),
        in_specs=[SCALARS] + [IN_HBM] * owners + [ANYWHERE] * len(after),
        out_specs=INSIDE,
        scratch_shapes=[pltpu.SMEM((owners, NOTE, 128), jnp.float32), pltpu.SemaphoreType.DMA(((PLANE + 1) * owners,))],
        cost_estimate=cost(micros),
    )(meta, *in_hbm(*sources), *after)


def places(offsets, sources, flipped):
    return [(offset, source, flipped) for source in sources for offset in offsets]


OTHERS = places((1, -1), range(4, 8), True) + places((2, -2), range(4, 8), True) + places((0,), range(4, 8), True)
OWNS = (
    places((3, -3, 4), range(8), False)
    + places((1, -1), range(4), True)
    + places((2, -2), range(4), True)
    + places((0,), range(4), True)
)


def prepare_kernel(owners, meta, slots, i0, i1, i2, i3, out_hi, out_lo, held, inverse, order, sems):
    per = ROW_TILES * TERM_SHARE
    g = pl.program_id(0)

    @pl.when(g == 0)
    def _():
        copies = [
            pltpu.make_async_copy(piece, held.at[pl.ds(n * per, per)], sems.at[n])
            for n, piece in enumerate((i0, i1, i2, i3))
        ]
        for copy in copies:
            copy.start()
        z, half, core = meta[0], meta[1], meta[2]
        mine = meta[3] * CO + core
        sign = 1 - 2 * core
        for n, (offset, source, flipped) in enumerate(owners):
            peer = source ^ (half * Y) if flipped else source
            order[n] = ((z - sign * offset) & (Z - 1)) * PLANE + peer

        def fill(k, carry):
            place = ((k >> 4) ^ mine) * per + (k & (TERM_SHARE - 1))
            for x in range(ROW_TILES):
                inverse[x, slots[x, k]] = place + x * TERM_SHARE
            return carry

        lax.fori_loop(0, OWNERS, fill, 0)
        for copy in copies:
            copy.wait()

    low = lax.broadcasted_iota(jnp.int32, (TILE // 2, 2 * TILE), 1) < TILE
    for pair in range(GROUP // 2):
        left, right = order[g * GROUP + 2 * pair], order[g * GROUP + 2 * pair + 1]
        for x in range(ROW_TILES):
            first = held[inverse[x, left]]
            second = held[inverse[x, right]]
            top = jnp.where(low, first, pltpu.roll(second, TILE, 1))
            bottom = jnp.where(low, pltpu.roll(first, TILE, 1), second)
            for half, value in enumerate((top, bottom)):
                hi, lo = split(value)
                rows = pl.ds(x * TILE + half * (TILE // 2), TILE // 2)
                cols = pl.ds(pair * 2 * TILE, 2 * TILE)
                out_hi[rows, cols] = hi
                out_lo[rows, cols] = lo


def prepare(owners, meta, slots, pieces, micros):
    rows, width = ROW_TILES * TILE, GROUP * TILE
    shape = jax.ShapeDtypeStruct((rows, len(owners) * TILE), jnp.bfloat16)
    block = pl.BlockSpec((rows, width), lambda g: (0, g))
    return pl.pallas_call(
        functools.partial(prepare_kernel, owners),
        grid=(len(owners) // GROUP,),
        out_shape=(shape, shape),
        in_specs=[SCALARS, SCALARS] + [ANYWHERE] * 4,
        out_specs=(block, block),
        scratch_shapes=[
            pltpu.VMEM((4 * ROW_TILES * TERM_SHARE, TILE // 2, 2 * TILE), jnp.float32),
            pltpu.SMEM((ROW_TILES, OWNERS), jnp.int32),
            pltpu.SMEM((OWNERS,), jnp.int32),
            pltpu.SemaphoreType.DMA((4,)),
        ],
        compiler_params=PARAMS,
        cost_estimate=cost(micros),
    )(meta, slots, *in_hbm(*pieces))


def product(left_hi, left_lo, right):
    hi, lo = split(right)
    total = jnp.dot(left_hi, lo, preferred_element_type=jnp.float32)
    total += jnp.dot(left_lo, hi, preferred_element_type=jnp.float32)
    return total + jnp.dot(left_hi, hi, preferred_element_type=jnp.float32)


def steps_kernel(count, meta, *refs):
    del meta
    tiles, lefts, out = refs[:count], refs[count : 3 * count], refs[3 * count]
    total = None
    for n in range(count):
        value = tiles[n][...].reshape(-1, tiles[n].shape[-1])
        term = product(lefts[2 * n][...], lefts[2 * n + 1][...], value)
        total = term if total is None else total + term
    out[...] = total


def full(x):
    return pl.BlockSpec(x.shape, lambda g: (0,) * x.ndim)


def steps(meta, tiles, offsets, part, left, micros):
    rows, cols = left[0].shape[0], tiles[0].shape[-1]
    shape = jax.ShapeDtypeStruct((rows, cols), jnp.float32)
    tile_specs, left_specs = [], []
    for t, offset in zip(tiles, offsets):
        depth = Y * t.shape[1] * TILE
        tile_specs.append(pl.BlockSpec((Y,) + t.shape[1:], lambda g, meta: (meta[1] ^ part, 0, 0, 0)))
        left_specs += [pl.BlockSpec((rows, depth), functools.partial(lambda i, g, meta: (0, i), offset // depth))] * 2
    return pl.pallas_call(
        functools.partial(steps_kernel, len(tiles)),
        out_shape=shape,
        grid_spec=pltpu.PrefetchScalarGridSpec(
            num_scalar_prefetch=1,
            grid=(1,),
            in_specs=tile_specs + left_specs,
            out_specs=pl.BlockSpec((rows, cols), lambda g, meta: (0, 0)),
        ),
        compiler_params=PARAMS,
        cost_estimate=cost(micros),
    )(meta, *tiles, *(list(left) * len(tiles)))


def last_kernel(tiles, left_hi, left_lo, total, other, amp, row_gap, col_gap, res, new):
    values = tiles[...].reshape(left_hi.shape[1], tiles.shape[-1])
    cycle = (total[...] + other[...] + product(left_hi[...], left_lo[...], values)).T
    column = jnp.broadcast_to(col_gap[...], (8, col_gap.shape[1])).T[:, :1]
    gap = column + row_gap[...]
    amplitudes = amp[...]
    residual = cycle - gap * amplitudes
    res[...] = residual
    new[...] = amplitudes + residual / gap


def last(offset, tiles, left, total, other, amp, row_gap, col_gap):
    rows, cols = left[0].shape[0], tiles.shape[-1]
    depth = PLANE * tiles.shape[1] * TILE
    block = pl.BlockSpec((rows, depth), lambda g: (0, offset // depth))
    shape = jax.ShapeDtypeStruct((cols, rows), jnp.float32)
    return pl.pallas_call(
        last_kernel,
        grid=(1,),
        out_shape=(shape, shape),
        in_specs=[full(tiles), block, block, full(total), full(other), full(amp), full(row_gap), full(col_gap)],
        out_specs=(full(shape), full(shape)),
        compiler_params=PARAMS,
    )(tiles, *left, total, other, amp, row_gap, col_gap)


def tie_kernel(*refs):
    del refs


def tie(xs, after):
    return pl.pallas_call(
        tie_kernel,
        compiler_params=PARAMS,
        out_shape=[jax.ShapeDtypeStruct(x.shape, x.dtype) for x in xs],
        in_specs=[IN_HBM] * len(xs) + [ANYWHERE] * len(after),
        out_specs=[IN_HBM] * len(xs),
        input_output_aliases={n: n for n in range(len(xs))},
    )(*in_hbm(*xs), *after)


def pack_kernel(integrals, after, out):
    del after
    value = integrals[0]
    out[...] = jnp.concatenate([value[:, : TILE // 2], value[:, TILE // 2 :]], axis=2)


def pack(integrals, after):
    shape = (TERM_SHARE, TILE // 2, 2 * TILE)
    return pl.pallas_call(
        pack_kernel,
        grid=(ROW_TILES,),
        compiler_params=PARAMS,
        out_shape=jax.ShapeDtypeStruct((ROW_TILES * TERM_SHARE,) + shape[1:], jnp.float32),
        in_specs=[pl.BlockSpec((1,) + integrals.shape[1:], lambda x: (x, 0, 0, 0)), IN_HBM],
        out_specs=pl.BlockSpec(shape, lambda x: (x, 0, 0)),
        cost_estimate=cost(PACK_COST),
    )(integrals, *in_hbm(after))


def swap(x, axis):
    return lax.ppermute(x, axis, [(0, 1), (1, 0)])


def shift(x, by):
    turns = [((z * CO + c), ((z + (by if c == 0 else -by)) % Z) * CO + c) for z in range(Z) for c in range(CO)]
    return lax.ppermute(x, ("z", "co"), turns)


def exchange(x, mirrored):
    if not mirrored:
        return lax.all_to_all(x, ("xh", "y"), 0, 0, tiled=True)
    groups = [[(xh * Y + y) * XL + (xh ^ d) for xh in range(XH) for y in range(Y)] for d in range(XL)]
    return lax.all_to_all(x, ("xh", "y", "xl"), 0, 0, axis_index_groups=groups, tiled=True)


def body(amplitudes, integrals, send_tiles, task_slots, row_gap, column_gap):
    meta = jnp.stack([lax.axis_index(n) for n in ("z", "xh", "co", "xl")]).astype(jnp.int32)
    owned = first(amplitudes, send_tiles)
    packed = pack(integrals, owned)
    across, beside = swap(packed, "xl"), swap(packed, "co")
    ring = {0: owned}
    received, chosen = [], []
    for n, (offsets, mirrored) in enumerate(zip(STEPS, MIRRORED)):
        after = [packed] if n == 0 else []
        if n > 0:
            ring[n], ring[-n] = shift(ring[n - 1], 1), shift(ring[1 - n], -1)
        if n > 1:
            ring[n], ring[-n] = tie([ring[n], ring[-n]], [received[n - 2]])
        if n == 3:
            ring[4] = shift(ring[3], 1)
            pieces = (packed, beside, across, swap(across, "co"))
            left = in_hbm(*prepare(OTHERS, meta, task_slots, pieces, PREPARE_COSTS[0]))
            after = left[:1]
        outgoing = select(meta, [ring[o] for o in offsets], after, SELECT_COST[n])
        chosen.append(outgoing)
        received.append(exchange(outgoing, mirrored))

    mirrored = [received[n] for n in (1, 2, 0)]
    other = steps(meta, mirrored, (0, 512, 1024), 1, left, OTHER_COST)
    pieces = (*tie([pieces[0]], [other]), *pieces[1:])
    other = swap(other, "xl")
    left = in_hbm(*prepare(OWNS, meta, task_slots, pieces, PREPARE_COSTS[1]))
    total = steps(meta, mirrored, (1536, 2048, 2560), 0, left, OWN_COST)
    return last(0, received[3], left, total, other, amplitudes, row_gap[None, :], column_gap[None, :])


def solution(mesh):
    fine = Mesh(mesh.devices.reshape(Z, XH, Y, XL, CO), ("z", "xh", "y", "xl", "co"))
    wide, narrow = ("z", "xh", "y"), ("xl", "co")
    return jax.shard_map(
        body,
        mesh=fine,
        in_specs=(P(narrow, wide), P(wide, narrow, None, None), P(wide, None), P(wide, None), P(wide), P(narrow)),
        out_specs=(P(narrow, wide), P(narrow, wide)),
        check_vma=False,
    )
```

```python
import functools

import jax
import jax.numpy as jnp
from jax import lax
from jax.experimental import pallas as pl
from jax.experimental.pallas import tpu as pltpu
from jax.sharding import Mesh, PartitionSpec as P

Z, XH, Y, XL, CO = 8, 2, 4, 2, 2
PLANE = XH * Y
OWNERS = Z * PLANE
TILE = 64
ROW_TILES = 8
TERM_SHARE = 16
GROUP = 4
NOTE = 8
SELECT_COST = (40, 40, 40, 15, 30)
PREPARE_COSTS = (10, 10)
MORE_COST = 60
PACK_COST = 40
PREPARE_COST = 10
OTHER_COST = 3
OWN_COST = 60
STEPS = ((0,), (1, -1), (2, -2), (3, -3), (4,))
MIRRORED = (True, True, True, False, False)
ANYWHERE = pl.BlockSpec(memory_space=pl.ANY)
IN_HBM = pl.BlockSpec(memory_space=pltpu.HBM)
INSIDE = pl.BlockSpec(memory_space=pltpu.VMEM)
SCALARS = pl.BlockSpec(memory_space=pltpu.SMEM)
PARAMS = pltpu.CompilerParams(vmem_limit_bytes=65500 * 1024)


def cost(micros):
    return pl.CostEstimate(flops=int(micros * 1e9), bytes_accessed=0, transcendentals=0)


def in_hbm(*xs):
    return [pltpu.with_memory_space_constraint(x, pltpu.HBM) for x in xs]


def split(x):
    hi = x.astype(jnp.bfloat16)
    lo = (x - hi.astype(jnp.float32)).astype(jnp.bfloat16)
    return hi, lo


def first_kernel(amp, send, out, held, sem):
    rows = amp.shape[1]
    held[pl.ds(0, rows)] = amp[...].T
    wide = jnp.pad(send[...].astype(jnp.float32), ((0, 0), (0, amp.shape[0] - OWNERS)))
    held[pl.ds(rows, NOTE)] = jnp.broadcast_to(wide, (NOTE, amp.shape[0]))
    copy = pltpu.make_async_copy(held, out, sem)
    copy.start()
    copy.wait()


def first(amp, send):
    cols, rows = amp.shape
    return pl.pallas_call(
        first_kernel,
        compiler_params=PARAMS,
        out_shape=jax.ShapeDtypeStruct((rows + NOTE, cols), jnp.float32),
        in_specs=[INSIDE, INSIDE],
        out_specs=IN_HBM,
        scratch_shapes=[pltpu.VMEM((rows + NOTE, cols), jnp.float32), pltpu.SemaphoreType.DMA],
    )(amp, send)


def select_kernel(owners, meta, *refs):
    sources, (out, notes, sems) = refs[:owners], refs[-3:]
    rows = ROW_TILES * TILE
    reads = [
        pltpu.make_async_copy(sources[n].at[pl.ds(rows, NOTE), pl.ds(0, 128)], notes.at[n], sems.at[PLANE * owners + n])
        for n in range(owners)
    ]
    for copy in reads:
        copy.start()
    copies = []
    for n in range(owners):
        reads[n].wait()
        for dest in range(PLANE):
            tile = jnp.clip(notes[n, 0, meta[0] * PLANE + dest].astype(jnp.int32), 0, ROW_TILES - 1)
            copy = pltpu.make_async_copy(
                sources[n].at[pl.ds(pl.multiple_of(tile * TILE, TILE), TILE)], out.at[dest, n], sems.at[n * PLANE + dest]
            )
            copy.start()
            copies.append(copy)
    for copy in copies:
        copy.wait()


def select(meta, sources, after, micros):
    owners, cols = len(sources), sources[0].shape[1]
    return pl.pallas_call(
        functools.partial(select_kernel, owners),
        compiler_params=PARAMS,
        out_shape=jax.ShapeDtypeStruct((PLANE, owners, TILE, cols), jnp.float32),
        in_specs=[SCALARS] + [IN_HBM] * owners + [ANYWHERE] * len(after),
        out_specs=INSIDE,
        scratch_shapes=[pltpu.SMEM((owners, NOTE, 128), jnp.float32), pltpu.SemaphoreType.DMA(((PLANE + 1) * owners,))],
        cost_estimate=cost(micros),
    )(meta, *in_hbm(*sources), *after)


def places(offsets, sources, flipped):
    return [(offset, source, flipped) for source in sources for offset in offsets]


OTHERS = places((1, -1), range(4, 8), True) + places((2, -2), range(4, 8), True) + places((0,), range(4, 8), True)
OWNS = (
    places((3, -3), range(8), False)
    + places((1, -1), range(4), True)
    + places((2, -2), range(4), True)
    + places((4,), range(8), False)
    + places((0,), range(4), True)
)


def prepare_kernel(owners, meta, slots, i0, i1, i2, i3, out_hi, out_lo, held, inverse, order, sems):
    per = ROW_TILES * TERM_SHARE
    g = pl.program_id(0)

    @pl.when(g == 0)
    def _():
        copies = [
            pltpu.make_async_copy(piece, held.at[pl.ds(n * per, per)], sems.at[n])
            for n, piece in enumerate((i0, i1, i2, i3))
        ]
        for copy in copies:
            copy.start()
        z, half, core = meta[0], meta[1], meta[2]
        mine = meta[3] * CO + core
        sign = 1 - 2 * core
        for n, (offset, source, flipped) in enumerate(owners):
            peer = source ^ (half * Y) if flipped else source
            order[n] = ((z - sign * offset) & (Z - 1)) * PLANE + peer

        def fill(k, carry):
            place = ((k >> 4) ^ mine) * per + (k & (TERM_SHARE - 1))
            for x in range(ROW_TILES):
                inverse[x, slots[x, k]] = place + x * TERM_SHARE
            return carry

        lax.fori_loop(0, OWNERS, fill, 0)
        for copy in copies:
            copy.wait()

    low = lax.broadcasted_iota(jnp.int32, (TILE // 2, 2 * TILE), 1) < TILE
    for pair in range(GROUP // 2):
        left, right = order[g * GROUP + 2 * pair], order[g * GROUP + 2 * pair + 1]
        for x in range(ROW_TILES):
            first = held[inverse[x, left]]
            second = held[inverse[x, right]]
            top = jnp.where(low, first, pltpu.roll(second, TILE, 1))
            bottom = jnp.where(low, pltpu.roll(first, TILE, 1), second)
            for half, value in enumerate((top, bottom)):
                hi, lo = split(value)
                rows = pl.ds(x * TILE + half * (TILE // 2), TILE // 2)
                cols = pl.ds(pair * 2 * TILE, 2 * TILE)
                out_hi[rows, cols] = hi
                out_lo[rows, cols] = lo


def prepare(owners, meta, slots, pieces, micros):
    rows, width = ROW_TILES * TILE, GROUP * TILE
    shape = jax.ShapeDtypeStruct((rows, len(owners) * TILE), jnp.bfloat16)
    block = pl.BlockSpec((rows, width), lambda g: (0, g))
    return pl.pallas_call(
        functools.partial(prepare_kernel, owners),
        grid=(len(owners) // GROUP,),
        out_shape=(shape, shape),
        in_specs=[SCALARS, SCALARS] + [ANYWHERE] * 4,
        out_specs=(block, block),
        scratch_shapes=[
            pltpu.VMEM((4 * ROW_TILES * TERM_SHARE, TILE // 2, 2 * TILE), jnp.float32),
            pltpu.SMEM((ROW_TILES, OWNERS), jnp.int32),
            pltpu.SMEM((OWNERS,), jnp.int32),
            pltpu.SemaphoreType.DMA((4,)),
        ],
        compiler_params=PARAMS,
        cost_estimate=cost(micros),
    )(meta, slots, *in_hbm(*pieces))


def product(left_hi, left_lo, right):
    hi, lo = split(right)
    total = jnp.dot(left_hi, lo, preferred_element_type=jnp.float32)
    total += jnp.dot(left_lo, hi, preferred_element_type=jnp.float32)
    return total + jnp.dot(left_hi, hi, preferred_element_type=jnp.float32)


def steps_kernel(count, meta, *refs):
    del meta
    tiles, lefts, out = refs[:count], refs[count : 3 * count], refs[3 * count]
    total = None
    for n in range(count):
        value = tiles[n][...].reshape(-1, tiles[n].shape[-1])
        term = product(lefts[2 * n][...], lefts[2 * n + 1][...], value)
        total = term if total is None else total + term
    out[...] = total


def full(x):
    return pl.BlockSpec(x.shape, lambda g: (0,) * x.ndim)


def steps(meta, tiles, offsets, part, left, micros):
    rows, cols = left[0].shape[0], tiles[0].shape[-1]
    shape = jax.ShapeDtypeStruct((rows, cols), jnp.float32)
    tile_specs, left_specs = [], []
    for t, offset in zip(tiles, offsets):
        depth = Y * t.shape[1] * TILE
        tile_specs.append(pl.BlockSpec((Y,) + t.shape[1:], lambda g, meta: (meta[1] ^ part, 0, 0, 0)))
        left_specs += [pl.BlockSpec((rows, depth), functools.partial(lambda i, g, meta: (0, i), offset // depth))] * 2
    return pl.pallas_call(
        functools.partial(steps_kernel, len(tiles)),
        out_shape=shape,
        grid_spec=pltpu.PrefetchScalarGridSpec(
            num_scalar_prefetch=1,
            grid=(1,),
            in_specs=tile_specs + left_specs,
            out_specs=pl.BlockSpec((rows, cols), lambda g, meta: (0, 0)),
        ),
        compiler_params=PARAMS,
        cost_estimate=cost(micros),
    )(meta, *tiles, *(list(left) * len(tiles)))


def last_kernel(tiles, left_hi, left_lo, total, other, amp, row_gap, col_gap, res, new):
    values = tiles[...].reshape(left_hi.shape[1], tiles.shape[-1])
    cycle = (total[...] + other[...] + product(left_hi[...], left_lo[...], values)).T
    column = jnp.broadcast_to(col_gap[...], (8, col_gap.shape[1])).T[:, :1]
    gap = column + row_gap[...]
    amplitudes = amp[...]
    residual = cycle - gap * amplitudes
    res[...] = residual
    new[...] = amplitudes + residual / gap


def last(offset, tiles, left, total, other, amp, row_gap, col_gap):
    rows, cols = left[0].shape[0], tiles.shape[-1]
    depth = PLANE * tiles.shape[1] * TILE
    block = pl.BlockSpec((rows, depth), lambda g: (0, offset // depth))
    shape = jax.ShapeDtypeStruct((cols, rows), jnp.float32)
    return pl.pallas_call(
        last_kernel,
        grid=(1,),
        out_shape=(shape, shape),
        in_specs=[full(tiles), block, block, full(total), full(other), full(amp), full(row_gap), full(col_gap)],
        out_specs=(full(shape), full(shape)),
        compiler_params=PARAMS,
    )(tiles, *left, total, other, amp, row_gap, col_gap)


def more_kernel(tiles, left_hi, left_lo, total, out):
    values = tiles[...].reshape(left_hi.shape[1], tiles.shape[-1])
    out[...] = total[...] + product(left_hi[...], left_lo[...], values)


def more(index, tiles, left, total, micros):
    rows = left[0].shape[0]
    block = pl.BlockSpec((rows, PLANE * tiles.shape[1] * TILE), lambda g: (0, index))
    return pl.pallas_call(
        more_kernel,
        grid=(1,),
        out_shape=jax.ShapeDtypeStruct(total.shape, jnp.float32),
        in_specs=[full(tiles), block, block, full(total)],
        out_specs=full(total),
        compiler_params=PARAMS,
        cost_estimate=cost(micros),
    )(tiles, *left, total)


def tie_kernel(*refs):
    del refs


def tie(xs, after):
    return pl.pallas_call(
        tie_kernel,
        compiler_params=PARAMS,
        out_shape=[jax.ShapeDtypeStruct(x.shape, x.dtype) for x in xs],
        in_specs=[IN_HBM] * len(xs) + [ANYWHERE] * len(after),
        out_specs=[IN_HBM] * len(xs),
        input_output_aliases={n: n for n in range(len(xs))},
        cost_estimate=cost(20),
    )(*in_hbm(*xs), *after)


def pack_kernel(integrals, after, out):
    del after
    value = integrals[0]
    out[...] = jnp.concatenate([value[:, : TILE // 2], value[:, TILE // 2 :]], axis=2)


def pack(integrals, after):
    shape = (TERM_SHARE, TILE // 2, 2 * TILE)
    return pl.pallas_call(
        pack_kernel,
        grid=(ROW_TILES,),
        compiler_params=PARAMS,
        out_shape=jax.ShapeDtypeStruct((ROW_TILES * TERM_SHARE,) + shape[1:], jnp.float32),
        in_specs=[pl.BlockSpec((1,) + integrals.shape[1:], lambda x: (x, 0, 0, 0)), IN_HBM],
        out_specs=pl.BlockSpec(shape, lambda x: (x, 0, 0)),
        cost_estimate=cost(PACK_COST),
    )(integrals, *in_hbm(after))


def swap(x, axis):
    return lax.ppermute(x, axis, [(0, 1), (1, 0)])


def shift(x, by):
    turns = [((z * CO + c), ((z + (by if c == 0 else -by)) % Z) * CO + c) for z in range(Z) for c in range(CO)]
    return lax.ppermute(x, ("z", "co"), turns)


def exchange(x, mirrored):
    if not mirrored:
        return lax.all_to_all(x, ("xh", "y"), 0, 0, tiled=True)
    groups = [[(xh * Y + y) * XL + (xh ^ d) for xh in range(XH) for y in range(Y)] for d in range(XL)]
    return lax.all_to_all(x, ("xh", "y", "xl"), 0, 0, axis_index_groups=groups, tiled=True)


def body(amplitudes, integrals, send_tiles, task_slots, row_gap, column_gap):
    meta = jnp.stack([lax.axis_index(n) for n in ("z", "xh", "co", "xl")]).astype(jnp.int32)
    owned = first(amplitudes, send_tiles)
    ring = {0: owned}
    received, chosen = [], []
    for n, (offsets, mirrored) in enumerate(zip(STEPS, MIRRORED)):
        after = []
        if n == Z // 2:
            ring[n] = shift(ring[n - 1], 1)
        elif n > 0:
            ring[n], ring[-n] = shift(ring[n - 1], 1), shift(ring[1 - n], -1)
        if n == 3:
            (across,) = tie([across], [received[1]])
        if 1 < n < Z // 2:
            ring[n], ring[-n] = tie([ring[n], ring[-n]], [received[n - 2]])
        if n == 3:
            pieces = (packed, beside, across, swap(across, "co"))
            left = in_hbm(*prepare(OTHERS, meta, task_slots, pieces, PREPARE_COSTS[0]))
        if n == Z // 2:
            after = left[:1]
        outgoing = select(meta, [ring[o] for o in offsets], after, SELECT_COST[n])
        if n == 0:
            packed = pack(integrals, outgoing)
            across, beside = swap(packed, "xl"), swap(packed, "co")
        chosen.append(outgoing)
        received.append(exchange(outgoing, mirrored))

    mirrored = [received[n] for n in (1, 2, 0)]
    other = steps(meta, mirrored, (0, 512, 1024), 1, left, OTHER_COST)
    pieces = (*tie([pieces[0]], [other]), *pieces[1:])
    other = swap(other, "xl")
    left = in_hbm(*prepare(OWNS, meta, task_slots, pieces, PREPARE_COSTS[1]))
    total = steps(meta, mirrored, (1024, 1536, 2560), 0, left, OWN_COST)
    total = more(0, received[3], left, total, MORE_COST)
    return last(2048, received[4], left, total, other, amplitudes, row_gap[None, :], column_gap[None, :])


def solution(mesh):
    fine = Mesh(mesh.devices.reshape(Z, XH, Y, XL, CO), ("z", "xh", "y", "xl", "co"))
    wide, narrow = ("z", "xh", "y"), ("xl", "co")
    return jax.shard_map(
        body,
        mesh=fine,
        in_specs=(P(narrow, wide), P(wide, narrow, None, None), P(wide, None), P(wide, None), P(wide), P(narrow)),
        out_specs=(P(narrow, wide), P(narrow, wide)),
        check_vma=False,
    )
```

```python
import functools

import jax
import jax.numpy as jnp
from jax import lax
from jax.experimental import pallas as pl
from jax.experimental.pallas import tpu as pltpu
from jax.sharding import Mesh, PartitionSpec as P

Z, XH, Y, XL, CO = 8, 2, 4, 2, 2
PLANE = XH * Y
OWNERS = Z * PLANE
TILE = 64
ROW_TILES = 8
TERM_SHARE = 16
GROUP = 4
NOTE = 8
SELECT_COST = (40, 40, 40, 15, 30)
PREPARE_COSTS = (10, 10)
MORE_COST = 60
PACK_COST = 40
PREPARE_COST = 10
OTHER_COST = 3
OWN_COST = 60
STEPS = ((0,), (1, -1), (2, -2), (3, -3), (4,))
MIRRORED = (True, True, True, False, False)
ANYWHERE = pl.BlockSpec(memory_space=pl.ANY)
IN_HBM = pl.BlockSpec(memory_space=pltpu.HBM)
INSIDE = pl.BlockSpec(memory_space=pltpu.VMEM)
SCALARS = pl.BlockSpec(memory_space=pltpu.SMEM)
PARAMS = pltpu.CompilerParams(vmem_limit_bytes=65500 * 1024)


def cost(micros):
    return pl.CostEstimate(flops=int(micros * 1e9), bytes_accessed=0, transcendentals=0)


def in_hbm(*xs):
    return [pltpu.with_memory_space_constraint(x, pltpu.HBM) for x in xs]


def split(x):
    hi = x.astype(jnp.bfloat16)
    lo = (x - hi.astype(jnp.float32)).astype(jnp.bfloat16)
    return hi, lo


def first_kernel(amp, send, out, held, sem):
    rows = amp.shape[1]
    held[pl.ds(0, rows)] = amp[...].T
    wide = jnp.pad(send[...].astype(jnp.float32), ((0, 0), (0, amp.shape[0] - OWNERS)))
    held[pl.ds(rows, NOTE)] = jnp.broadcast_to(wide, (NOTE, amp.shape[0]))
    copy = pltpu.make_async_copy(held, out, sem)
    copy.start()
    copy.wait()


def first(amp, send):
    cols, rows = amp.shape
    return pl.pallas_call(
        first_kernel,
        compiler_params=PARAMS,
        out_shape=jax.ShapeDtypeStruct((rows + NOTE, cols), jnp.float32),
        in_specs=[INSIDE, INSIDE],
        out_specs=IN_HBM,
        scratch_shapes=[pltpu.VMEM((rows + NOTE, cols), jnp.float32), pltpu.SemaphoreType.DMA],
    )(amp, send)


def select_kernel(owners, meta, *refs):
    sources, (out, notes, sems) = refs[:owners], refs[-3:]
    rows = ROW_TILES * TILE
    reads = [
        pltpu.make_async_copy(sources[n].at[pl.ds(rows, NOTE), pl.ds(0, 128)], notes.at[n], sems.at[PLANE * owners + n])
        for n in range(owners)
    ]
    for copy in reads:
        copy.start()
    copies = []
    for n in range(owners):
        reads[n].wait()
        for dest in range(PLANE):
            tile = jnp.clip(notes[n, 0, meta[0] * PLANE + dest].astype(jnp.int32), 0, ROW_TILES - 1)
            copy = pltpu.make_async_copy(
                sources[n].at[pl.ds(pl.multiple_of(tile * TILE, TILE), TILE)], out.at[dest, n], sems.at[n * PLANE + dest]
            )
            copy.start()
            copies.append(copy)
    for copy in copies:
        copy.wait()


def select(meta, sources, after, micros):
    owners, cols = len(sources), sources[0].shape[1]
    return pl.pallas_call(
        functools.partial(select_kernel, owners),
        compiler_params=PARAMS,
        out_shape=jax.ShapeDtypeStruct((PLANE, owners, TILE, cols), jnp.float32),
        in_specs=[SCALARS] + [IN_HBM] * owners + [ANYWHERE] * len(after),
        out_specs=INSIDE,
        scratch_shapes=[pltpu.SMEM((owners, NOTE, 128), jnp.float32), pltpu.SemaphoreType.DMA(((PLANE + 1) * owners,))],
        cost_estimate=cost(micros),
    )(meta, *in_hbm(*sources), *after)


def scatter_kernel(meta, source, *refs):
    outs, notes, sems = refs[-PLANE - 2 : -2], refs[-2], refs[-1]
    rows = ROW_TILES * TILE
    read = pltpu.make_async_copy(source.at[pl.ds(rows, NOTE), pl.ds(0, 128)], notes, sems.at[PLANE])
    read.start()
    read.wait()
    copies = []
    for n, out in enumerate(outs):
        reader = meta[0] * PLANE + (meta[1] ^ (n // Y)) * Y + ((meta[4] + n % Y) & (Y - 1))
        tile = jnp.clip(notes[0, reader].astype(jnp.int32), 0, ROW_TILES - 1)
        copy = pltpu.make_async_copy(source.at[pl.ds(pl.multiple_of(tile * TILE, TILE), TILE)], out, sems.at[n])
        copy.start()
        copies.append(copy)
    for copy in copies:
        copy.wait()


def scatter(meta, source, after, micros):
    shape = jax.ShapeDtypeStruct((TILE, source.shape[1]), jnp.float32)
    return pl.pallas_call(
        scatter_kernel,
        compiler_params=PARAMS,
        out_shape=[shape] * PLANE,
        in_specs=[SCALARS, IN_HBM] + [ANYWHERE] * len(after),
        out_specs=[INSIDE] * PLANE,
        scratch_shapes=[pltpu.SMEM((NOTE, 128), jnp.float32), pltpu.SemaphoreType.DMA((PLANE + 1,))],
        cost_estimate=cost(micros),
    )(meta, *in_hbm(source), *after)


def places(offsets, sources, flipped):
    return [(offset, source, flipped) for source in sources for offset in offsets]


OTHERS = places((1, -1), range(4, 8), True) + places((2, -2), range(4, 8), True) + places((0,), range(4, 8), True)
OWNS = (
    places((3, -3), range(8), False)
    + places((1, -1), range(4), True)
    + places((2, -2), range(4), True)
    + places((4,), range(8), None)
    + places((0,), range(4), True)
)


def prepare_kernel(owners, meta, slots, i0, i1, i2, i3, out_hi, out_lo, held, inverse, order, sems):
    per = ROW_TILES * TERM_SHARE
    g = pl.program_id(0)

    @pl.when(g == 0)
    def _():
        copies = [
            pltpu.make_async_copy(piece, held.at[pl.ds(n * per, per)], sems.at[n])
            for n, piece in enumerate((i0, i1, i2, i3))
        ]
        for copy in copies:
            copy.start()
        z, half, core = meta[0], meta[1], meta[2]
        mine = meta[3] * CO + core
        sign = 1 - 2 * core
        for n, (offset, source, flipped) in enumerate(owners):
            if flipped is None:
                peer = (half ^ (source // Y)) * Y + ((meta[4] - source % Y) & (Y - 1))
            else:
                peer = source ^ (half * Y) if flipped else source
            order[n] = ((z - sign * offset) & (Z - 1)) * PLANE + peer

        def fill(k, carry):
            place = ((k >> 4) ^ mine) * per + (k & (TERM_SHARE - 1))
            for x in range(ROW_TILES):
                inverse[x, slots[x, k]] = place + x * TERM_SHARE
            return carry

        lax.fori_loop(0, OWNERS, fill, 0)
        for copy in copies:
            copy.wait()

    low = lax.broadcasted_iota(jnp.int32, (TILE // 2, 2 * TILE), 1) < TILE
    for pair in range(GROUP // 2):
        left, right = order[g * GROUP + 2 * pair], order[g * GROUP + 2 * pair + 1]
        for x in range(ROW_TILES):
            first = held[inverse[x, left]]
            second = held[inverse[x, right]]
            top = jnp.where(low, first, pltpu.roll(second, TILE, 1))
            bottom = jnp.where(low, pltpu.roll(first, TILE, 1), second)
            for half, value in enumerate((top, bottom)):
                hi, lo = split(value)
                rows = pl.ds(x * TILE + half * (TILE // 2), TILE // 2)
                cols = pl.ds(pair * 2 * TILE, 2 * TILE)
                out_hi[rows, cols] = hi
                out_lo[rows, cols] = lo


def prepare(owners, meta, slots, pieces, micros):
    rows, width = ROW_TILES * TILE, GROUP * TILE
    shape = jax.ShapeDtypeStruct((rows, len(owners) * TILE), jnp.bfloat16)
    block = pl.BlockSpec((rows, width), lambda g: (0, g))
    return pl.pallas_call(
        functools.partial(prepare_kernel, owners),
        grid=(len(owners) // GROUP,),
        out_shape=(shape, shape),
        in_specs=[SCALARS, SCALARS] + [ANYWHERE] * 4,
        out_specs=(block, block),
        scratch_shapes=[
            pltpu.VMEM((4 * ROW_TILES * TERM_SHARE, TILE // 2, 2 * TILE), jnp.float32),
            pltpu.SMEM((ROW_TILES, OWNERS), jnp.int32),
            pltpu.SMEM((OWNERS,), jnp.int32),
            pltpu.SemaphoreType.DMA((4,)),
        ],
        compiler_params=PARAMS,
        cost_estimate=cost(micros),
    )(meta, slots, *in_hbm(*pieces))


def product(left_hi, left_lo, right):
    hi, lo = split(right)
    total = jnp.dot(left_hi, lo, preferred_element_type=jnp.float32)
    total += jnp.dot(left_lo, hi, preferred_element_type=jnp.float32)
    return total + jnp.dot(left_hi, hi, preferred_element_type=jnp.float32)


def steps_kernel(count, meta, *refs):
    del meta
    tiles, lefts, out = refs[:count], refs[count : 3 * count], refs[3 * count]
    total = None
    for n in range(count):
        value = tiles[n][...].reshape(-1, tiles[n].shape[-1])
        term = product(lefts[2 * n][...], lefts[2 * n + 1][...], value)
        total = term if total is None else total + term
    out[...] = total


def full(x):
    return pl.BlockSpec(x.shape, lambda g: (0,) * x.ndim)


def steps(meta, tiles, offsets, part, left, micros):
    rows, cols = left[0].shape[0], tiles[0].shape[-1]
    shape = jax.ShapeDtypeStruct((rows, cols), jnp.float32)
    tile_specs, left_specs = [], []
    for t, offset in zip(tiles, offsets):
        depth = Y * t.shape[1] * TILE
        tile_specs.append(pl.BlockSpec((Y,) + t.shape[1:], lambda g, meta: (meta[1] ^ part, 0, 0, 0)))
        left_specs += [pl.BlockSpec((rows, depth), functools.partial(lambda i, g, meta: (0, i), offset // depth))] * 2
    return pl.pallas_call(
        functools.partial(steps_kernel, len(tiles)),
        out_shape=shape,
        grid_spec=pltpu.PrefetchScalarGridSpec(
            num_scalar_prefetch=1,
            grid=(1,),
            in_specs=tile_specs + left_specs,
            out_specs=pl.BlockSpec((rows, cols), lambda g, meta: (0, 0)),
        ),
        compiler_params=PARAMS,
        cost_estimate=cost(micros),
    )(meta, *tiles, *(list(left) * len(tiles)))


def last_kernel(*refs):
    tiles, refs = refs[:PLANE], refs[PLANE:]
    left_hi, left_lo, total, other, amp, row_gap, col_gap, res, new = refs
    values = jnp.concatenate([tile[...] for tile in tiles], axis=0)
    cycle = (total[...] + other[...] + product(left_hi[...], left_lo[...], values)).T
    column = jnp.broadcast_to(col_gap[...], (8, col_gap.shape[1])).T[:, :1]
    gap = column + row_gap[...]
    amplitudes = amp[...]
    residual = cycle - gap * amplitudes
    res[...] = residual
    new[...] = amplitudes + residual / gap


def last(offset, tiles, left, total, other, amp, row_gap, col_gap):
    cols, rows = amp.shape
    depth = PLANE * TILE
    block = pl.BlockSpec((rows, depth), lambda g: (0, offset // depth))
    shape = jax.ShapeDtypeStruct((cols, rows), jnp.float32)
    rest = (total, other, amp, row_gap, col_gap)
    return pl.pallas_call(
        last_kernel,
        grid=(1,),
        out_shape=(shape, shape),
        in_specs=[full(t) for t in tiles] + [block, block] + [full(x) for x in rest],
        out_specs=(full(shape), full(shape)),
        compiler_params=PARAMS,
    )(*tiles, *left, *rest)


def more_kernel(tiles, left_hi, left_lo, total, out):
    values = tiles[...].reshape(left_hi.shape[1], tiles.shape[-1])
    out[...] = total[...] + product(left_hi[...], left_lo[...], values)


def more(index, tiles, left, total, micros):
    rows = left[0].shape[0]
    block = pl.BlockSpec((rows, PLANE * tiles.shape[1] * TILE), lambda g: (0, index))
    return pl.pallas_call(
        more_kernel,
        grid=(1,),
        out_shape=jax.ShapeDtypeStruct(total.shape, jnp.float32),
        in_specs=[full(tiles), block, block, full(total)],
        out_specs=full(total),
        compiler_params=PARAMS,
        cost_estimate=cost(micros),
    )(tiles, *left, total)


def tie_kernel(*refs):
    del refs


def tie(xs, after):
    return pl.pallas_call(
        tie_kernel,
        compiler_params=PARAMS,
        out_shape=[jax.ShapeDtypeStruct(x.shape, x.dtype) for x in xs],
        in_specs=[IN_HBM] * len(xs) + [ANYWHERE] * len(after),
        out_specs=[IN_HBM] * len(xs),
        input_output_aliases={n: n for n in range(len(xs))},
        cost_estimate=cost(20),
    )(*in_hbm(*xs), *after)


def pack_kernel(integrals, after, out):
    del after
    value = integrals[0]
    out[...] = jnp.concatenate([value[:, : TILE // 2], value[:, TILE // 2 :]], axis=2)


def pack(integrals, after):
    shape = (TERM_SHARE, TILE // 2, 2 * TILE)
    return pl.pallas_call(
        pack_kernel,
        grid=(ROW_TILES,),
        compiler_params=PARAMS,
        out_shape=jax.ShapeDtypeStruct((ROW_TILES * TERM_SHARE,) + shape[1:], jnp.float32),
        in_specs=[pl.BlockSpec((1,) + integrals.shape[1:], lambda x: (x, 0, 0, 0)), IN_HBM],
        out_specs=pl.BlockSpec(shape, lambda x: (x, 0, 0)),
        cost_estimate=cost(PACK_COST),
    )(integrals, *in_hbm(after))


def swap(x, axis):
    return lax.ppermute(x, axis, [(0, 1), (1, 0)])


def shift(x, by):
    turns = [((z * CO + c), ((z + (by if c == 0 else -by)) % Z) * CO + c) for z in range(Z) for c in range(CO)]
    return lax.ppermute(x, ("z", "co"), turns)


def send(x, n):
    if n == 0:
        return x
    turns = [(xh * Y + y, (xh ^ (n // Y)) * Y + (y + n % Y) % Y) for xh in range(XH) for y in range(Y)]
    return lax.ppermute(x, ("xh", "y"), turns)


def exchange(x, mirrored):
    if not mirrored:
        return lax.all_to_all(x, ("xh", "y"), 0, 0, tiled=True)
    groups = [[(xh * Y + y) * XL + (xh ^ d) for xh in range(XH) for y in range(Y)] for d in range(XL)]
    return lax.all_to_all(x, ("xh", "y", "xl"), 0, 0, axis_index_groups=groups, tiled=True)


def body(amplitudes, integrals, send_tiles, task_slots, row_gap, column_gap):
    meta = jnp.stack([lax.axis_index(n) for n in ("z", "xh", "co", "xl", "y")]).astype(jnp.int32)
    owned = first(amplitudes, send_tiles)
    ring = {0: owned}
    received, chosen = [], []
    for n, (offsets, mirrored) in enumerate(zip(STEPS, MIRRORED)):
        after = []
        if n == Z // 2:
            ring[n] = shift(ring[n - 1], 1)
        elif n > 0:
            ring[n], ring[-n] = shift(ring[n - 1], 1), shift(ring[1 - n], -1)
        if n == 3:
            (across,) = tie([across], [received[1]])
        if 1 < n < Z // 2:
            ring[n], ring[-n] = tie([ring[n], ring[-n]], [received[n - 2]])
        if n == 3:
            pieces = (packed, beside, across, swap(across, "co"))
            left = in_hbm(*prepare(OTHERS, meta, task_slots, pieces, PREPARE_COSTS[0]))
        if n == Z // 2:
            after = left[:1]
            apart = scatter(meta, ring[n], after, SELECT_COST[n])
            received.append([send(x, r) for r, x in enumerate(apart)])
            break
        outgoing = select(meta, [ring[o] for o in offsets], after, SELECT_COST[n])
        if n == 0:
            packed = pack(integrals, outgoing)
            across, beside = swap(packed, "xl"), swap(packed, "co")
        chosen.append(outgoing)
        received.append(exchange(outgoing, mirrored))

    mirrored = [received[n] for n in (1, 2, 0)]
    other = steps(meta, mirrored, (0, 512, 1024), 1, left, OTHER_COST)
    pieces = (*tie([pieces[0]], [other]), *pieces[1:])
    other = swap(other, "xl")
    left = in_hbm(*prepare(OWNS, meta, task_slots, pieces, PREPARE_COSTS[1]))
    total = steps(meta, mirrored, (1024, 1536, 2560), 0, left, OWN_COST)
    total = more(0, received[3], left, total, MORE_COST)
    return last(2048, received[4], left, total, other, amplitudes, row_gap[None, :], column_gap[None, :])


def solution(mesh):
    fine = Mesh(mesh.devices.reshape(Z, XH, Y, XL, CO), ("z", "xh", "y", "xl", "co"))
    wide, narrow = ("z", "xh", "y"), ("xl", "co")
    return jax.shard_map(
        body,
        mesh=fine,
        in_specs=(P(narrow, wide), P(wide, narrow, None, None), P(wide, None), P(wide, None), P(wide), P(narrow)),
        out_specs=(P(narrow, wide), P(narrow, wide)),
        check_vma=False,
    )
```

```python
import functools

import jax
import jax.numpy as jnp
from jax import lax
from jax.experimental import pallas as pl
from jax.experimental.pallas import tpu as pltpu
from jax.sharding import Mesh, PartitionSpec as P

Z, XH, Y, XL, CO = 8, 2, 4, 2, 2
PLANE = XH * Y
OWNERS = Z * PLANE
TILE = 64
ROW_TILES = 8
TERM_SHARE = 16
GROUP = 4
NOTE = 8
SELECT_COST = (40, 40, 40, 15, 30)
PREPARE_COSTS = (10, 10)
MORE_COST = 60
PACK_COST = 40
PREPARE_COST = 10
OTHER_COST = 3
OWN_COST = 60
STEPS = ((0,), (1, -1), (2, -2), (3, -3), (4,))
MIRRORED = (True, True, True, False, False)
ANYWHERE = pl.BlockSpec(memory_space=pl.ANY)
IN_HBM = pl.BlockSpec(memory_space=pltpu.HBM)
INSIDE = pl.BlockSpec(memory_space=pltpu.VMEM)
SCALARS = pl.BlockSpec(memory_space=pltpu.SMEM)
PARAMS = pltpu.CompilerParams(vmem_limit_bytes=65500 * 1024)


def cost(micros):
    return pl.CostEstimate(flops=int(micros * 1e9), bytes_accessed=0, transcendentals=0)


def in_hbm(*xs):
    return [pltpu.with_memory_space_constraint(x, pltpu.HBM) for x in xs]


def split(x):
    hi = x.astype(jnp.bfloat16)
    lo = (x - hi.astype(jnp.float32)).astype(jnp.bfloat16)
    return hi, lo


def first_kernel(amp, send, out, held, sem):
    rows = amp.shape[1]
    held[pl.ds(0, rows)] = amp[...].T
    wide = jnp.pad(send[...].astype(jnp.float32), ((0, 0), (0, amp.shape[0] - OWNERS)))
    held[pl.ds(rows, NOTE)] = jnp.broadcast_to(wide, (NOTE, amp.shape[0]))
    copy = pltpu.make_async_copy(held, out, sem)
    copy.start()
    copy.wait()


def first(amp, send):
    cols, rows = amp.shape
    return pl.pallas_call(
        first_kernel,
        compiler_params=PARAMS,
        out_shape=jax.ShapeDtypeStruct((rows + NOTE, cols), jnp.float32),
        in_specs=[INSIDE, INSIDE],
        out_specs=IN_HBM,
        scratch_shapes=[pltpu.VMEM((rows + NOTE, cols), jnp.float32), pltpu.SemaphoreType.DMA],
    )(amp, send)


def select_kernel(owners, meta, *refs):
    sources, (out, notes, sems) = refs[:owners], refs[-3:]
    rows = ROW_TILES * TILE
    reads = [
        pltpu.make_async_copy(sources[n].at[pl.ds(rows, NOTE), pl.ds(0, 128)], notes.at[n], sems.at[PLANE * owners + n])
        for n in range(owners)
    ]
    for copy in reads:
        copy.start()
    copies = []
    for n in range(owners):
        reads[n].wait()
        for dest in range(PLANE):
            tile = jnp.clip(notes[n, 0, meta[0] * PLANE + dest].astype(jnp.int32), 0, ROW_TILES - 1)
            copy = pltpu.make_async_copy(
                sources[n].at[pl.ds(pl.multiple_of(tile * TILE, TILE), TILE)], out.at[dest, n], sems.at[n * PLANE + dest]
            )
            copy.start()
            copies.append(copy)
    for copy in copies:
        copy.wait()


def select(meta, sources, after, micros):
    owners, cols = len(sources), sources[0].shape[1]
    return pl.pallas_call(
        functools.partial(select_kernel, owners),
        compiler_params=PARAMS,
        out_shape=jax.ShapeDtypeStruct((PLANE, owners, TILE, cols), jnp.float32),
        in_specs=[SCALARS] + [IN_HBM] * owners + [ANYWHERE] * len(after),
        out_specs=INSIDE,
        scratch_shapes=[pltpu.SMEM((owners, NOTE, 128), jnp.float32), pltpu.SemaphoreType.DMA(((PLANE + 1) * owners,))],
        cost_estimate=cost(micros),
    )(meta, *in_hbm(*sources), *after)


def scatter_kernel(meta, source, *refs):
    outs, notes, sems = refs[-PLANE - 2 : -2], refs[-2], refs[-1]
    rows = ROW_TILES * TILE
    read = pltpu.make_async_copy(source.at[pl.ds(rows, NOTE), pl.ds(0, 128)], notes, sems.at[PLANE])
    read.start()
    read.wait()
    copies = []
    for n, out in enumerate(outs):
        reader = meta[0] * PLANE + (meta[1] ^ (n // Y)) * Y + ((meta[4] + n % Y) & (Y - 1))
        tile = jnp.clip(notes[0, reader].astype(jnp.int32), 0, ROW_TILES - 1)
        copy = pltpu.make_async_copy(source.at[pl.ds(pl.multiple_of(tile * TILE, TILE), TILE)], out, sems.at[n])
        copy.start()
        copies.append(copy)
    for copy in copies:
        copy.wait()


def scatter(meta, source, after, micros):
    shape = jax.ShapeDtypeStruct((TILE, source.shape[1]), jnp.float32)
    return pl.pallas_call(
        scatter_kernel,
        compiler_params=PARAMS,
        out_shape=[shape] * PLANE,
        in_specs=[SCALARS, IN_HBM] + [ANYWHERE] * len(after),
        out_specs=[INSIDE] * PLANE,
        scratch_shapes=[pltpu.SMEM((NOTE, 128), jnp.float32), pltpu.SemaphoreType.DMA((PLANE + 1,))],
        cost_estimate=cost(micros),
    )(meta, *in_hbm(source), *after)


def places(offsets, sources, flipped):
    return [(offset, source, flipped) for source in sources for offset in offsets]


OTHERS = places((1, -1), range(4, 8), True) + places((2, -2), range(4, 8), True) + places((0,), range(4, 8), True)
OWNS = (
    places((3, -3), range(8), False)
    + places((1, -1), range(4), True)
    + places((2, -2), range(4), True)
    + places((4,), range(8), None)
    + places((0,), range(4), True)
)


def prepare_kernel(owners, meta, slots, i0, i1, i2, i3, out_hi, out_lo, held, inverse, order, sems):
    per = ROW_TILES * TERM_SHARE
    g = pl.program_id(0)

    @pl.when(g == 0)
    def _():
        copies = [
            pltpu.make_async_copy(piece, held.at[pl.ds(n * per, per)], sems.at[n])
            for n, piece in enumerate((i0, i1, i2, i3))
        ]
        for copy in copies:
            copy.start()
        z, half, core = meta[0], meta[1], meta[2]
        mine = meta[3] * CO + core
        sign = 1 - 2 * core
        for n, (offset, source, flipped) in enumerate(owners):
            if flipped is None:
                peer = (half ^ (source // Y)) * Y + ((meta[4] - source % Y) & (Y - 1))
            else:
                peer = source ^ (half * Y) if flipped else source
            order[n] = ((z - sign * offset) & (Z - 1)) * PLANE + peer

        def fill(k, carry):
            place = ((k >> 4) ^ mine) * per + (k & (TERM_SHARE - 1))
            for x in range(ROW_TILES):
                inverse[x, slots[x, k]] = place + x * TERM_SHARE
            return carry

        lax.fori_loop(0, OWNERS, fill, 0)
        for copy in copies:
            copy.wait()

    low = lax.broadcasted_iota(jnp.int32, (TILE // 2, 2 * TILE), 1) < TILE
    for pair in range(GROUP // 2):
        left, right = order[g * GROUP + 2 * pair], order[g * GROUP + 2 * pair + 1]
        for x in range(ROW_TILES):
            first = held[inverse[x, left]]
            second = held[inverse[x, right]]
            top = jnp.where(low, first, pltpu.roll(second, TILE, 1))
            bottom = jnp.where(low, pltpu.roll(first, TILE, 1), second)
            for half, value in enumerate((top, bottom)):
                hi, lo = split(value)
                rows = pl.ds(x * TILE + half * (TILE // 2), TILE // 2)
                cols = pl.ds(pair * 2 * TILE, 2 * TILE)
                out_hi[rows, cols] = hi
                out_lo[rows, cols] = lo


def prepare(owners, meta, slots, pieces, micros):
    rows, width = ROW_TILES * TILE, GROUP * TILE
    shape = jax.ShapeDtypeStruct((rows, len(owners) * TILE), jnp.bfloat16)
    block = pl.BlockSpec((rows, width), lambda g: (0, g))
    return pl.pallas_call(
        functools.partial(prepare_kernel, owners),
        grid=(len(owners) // GROUP,),
        out_shape=(shape, shape),
        in_specs=[SCALARS, SCALARS] + [ANYWHERE] * 4,
        out_specs=(block, block),
        scratch_shapes=[
            pltpu.VMEM((4 * ROW_TILES * TERM_SHARE, TILE // 2, 2 * TILE), jnp.float32),
            pltpu.SMEM((ROW_TILES, OWNERS), jnp.int32),
            pltpu.SMEM((OWNERS,), jnp.int32),
            pltpu.SemaphoreType.DMA((4,)),
        ],
        compiler_params=PARAMS,
        cost_estimate=cost(micros),
    )(meta, slots, *in_hbm(*pieces))


def product(left_hi, left_lo, right):
    hi, lo = split(right)
    total = jnp.dot(left_hi, lo, preferred_element_type=jnp.float32)
    total += jnp.dot(left_lo, hi, preferred_element_type=jnp.float32)
    return total + jnp.dot(left_hi, hi, preferred_element_type=jnp.float32)


def steps_kernel(count, meta, *refs):
    del meta
    tiles, lefts, out = refs[:count], refs[count : 3 * count], refs[3 * count]
    total = None
    for n in range(count):
        value = tiles[n][...].reshape(-1, tiles[n].shape[-1])
        term = product(lefts[2 * n][...], lefts[2 * n + 1][...], value)
        total = term if total is None else total + term
    out[...] = total


def full(x):
    return pl.BlockSpec(x.shape, lambda g: (0,) * x.ndim)


def steps(meta, tiles, offsets, part, left, micros):
    rows, cols = left[0].shape[0], tiles[0].shape[-1]
    shape = jax.ShapeDtypeStruct((rows, cols), jnp.float32)
    tile_specs, left_specs = [], []
    for t, offset in zip(tiles, offsets):
        depth = Y * t.shape[1] * TILE
        tile_specs.append(pl.BlockSpec((Y,) + t.shape[1:], lambda g, meta: (meta[1] ^ part, 0, 0, 0)))
        left_specs += [pl.BlockSpec((rows, depth), functools.partial(lambda i, g, meta: (0, i), offset // depth))] * 2
    return pl.pallas_call(
        functools.partial(steps_kernel, len(tiles)),
        out_shape=shape,
        grid_spec=pltpu.PrefetchScalarGridSpec(
            num_scalar_prefetch=1,
            grid=(1,),
            in_specs=tile_specs + left_specs,
            out_specs=pl.BlockSpec((rows, cols), lambda g, meta: (0, 0)),
        ),
        compiler_params=PARAMS,
        cost_estimate=cost(micros),
    )(meta, *tiles, *(list(left) * len(tiles)))


def last_kernel(meta, *refs):
    del meta
    far, third, near, refs = refs[:PLANE], refs[PLANE], refs[PLANE + 1 : PLANE + 4], refs[PLANE + 4 :]
    left_hi, left_lo, other, amp, row_gap, col_gap, res, new = refs
    cols = amp.shape[0]
    blocks = [third[...].reshape(-1, cols), near[0][...].reshape(-1, cols), near[1][...].reshape(-1, cols)]
    blocks += [jnp.concatenate([tile[...] for tile in far], axis=0), near[2][...].reshape(-1, cols)]
    total, start = other[...], 0
    for block in blocks:
        part = pl.ds(start, block.shape[0])
        total = total + product(left_hi[:, part], left_lo[:, part], block)
        start += block.shape[0]
    cycle = total.T
    column = jnp.broadcast_to(col_gap[...], (8, col_gap.shape[1])).T[:, :1]
    gap = column + row_gap[...]
    amplitudes = amp[...]
    residual = cycle - gap * amplitudes
    res[...] = residual
    new[...] = amplitudes + residual / gap


def last(meta, far, third, near, left, other, amp, row_gap, col_gap):
    shape = jax.ShapeDtypeStruct(amp.shape, jnp.float32)
    rest = (*left, other, amp, row_gap, col_gap)

    def whole(x):
        return pl.BlockSpec(x.shape, lambda g, meta: (0,) * x.ndim)

    halves = [pl.BlockSpec((Y,) + t.shape[1:], lambda g, meta: (meta[1], 0, 0, 0)) for t in near]
    return pl.pallas_call(
        last_kernel,
        out_shape=(shape, shape),
        grid_spec=pltpu.PrefetchScalarGridSpec(
            num_scalar_prefetch=1,
            grid=(1,),
            in_specs=[whole(x) for x in (*far, third)] + halves + [whole(x) for x in rest],
            out_specs=(whole(amp), whole(amp)),
        ),
        compiler_params=PARAMS,
    )(meta, *far, third, *near, *rest)


def tie_kernel(*refs):
    del refs


def tie(xs, after):
    return pl.pallas_call(
        tie_kernel,
        compiler_params=PARAMS,
        out_shape=[jax.ShapeDtypeStruct(x.shape, x.dtype) for x in xs],
        in_specs=[IN_HBM] * len(xs) + [ANYWHERE] * len(after),
        out_specs=[IN_HBM] * len(xs),
        input_output_aliases={n: n for n in range(len(xs))},
        cost_estimate=cost(20),
    )(*in_hbm(*xs), *after)


def pack_kernel(integrals, after, out):
    del after
    value = integrals[0]
    out[...] = jnp.concatenate([value[:, : TILE // 2], value[:, TILE // 2 :]], axis=2)


def pack(integrals, after):
    shape = (TERM_SHARE, TILE // 2, 2 * TILE)
    return pl.pallas_call(
        pack_kernel,
        grid=(ROW_TILES,),
        compiler_params=PARAMS,
        out_shape=jax.ShapeDtypeStruct((ROW_TILES * TERM_SHARE,) + shape[1:], jnp.float32),
        in_specs=[pl.BlockSpec((1,) + integrals.shape[1:], lambda x: (x, 0, 0, 0)), IN_HBM],
        out_specs=pl.BlockSpec(shape, lambda x: (x, 0, 0)),
        cost_estimate=cost(PACK_COST),
    )(integrals, *in_hbm(after))


def swap(x, axis):
    return lax.ppermute(x, axis, [(0, 1), (1, 0)])


def shift(x, by):
    turns = [((z * CO + c), ((z + (by if c == 0 else -by)) % Z) * CO + c) for z in range(Z) for c in range(CO)]
    return lax.ppermute(x, ("z", "co"), turns)


def send(x, n):
    if n == 0:
        return x
    turns = [(xh * Y + y, (xh ^ (n // Y)) * Y + (y + n % Y) % Y) for xh in range(XH) for y in range(Y)]
    return lax.ppermute(x, ("xh", "y"), turns)


def exchange(x, mirrored):
    if not mirrored:
        return lax.all_to_all(x, ("xh", "y"), 0, 0, tiled=True)
    groups = [[(xh * Y + y) * XL + (xh ^ d) for xh in range(XH) for y in range(Y)] for d in range(XL)]
    return lax.all_to_all(x, ("xh", "y", "xl"), 0, 0, axis_index_groups=groups, tiled=True)


def body(amplitudes, integrals, send_tiles, task_slots, row_gap, column_gap):
    meta = jnp.stack([lax.axis_index(n) for n in ("z", "xh", "co", "xl", "y")]).astype(jnp.int32)
    owned = first(amplitudes, send_tiles)
    ring = {0: owned}
    received, chosen = [], []
    for n, (offsets, mirrored) in enumerate(zip(STEPS, MIRRORED)):
        after = []
        if n == Z // 2:
            ring[n] = shift(ring[n - 1], 1)
        elif n > 0:
            ring[n], ring[-n] = shift(ring[n - 1], 1), shift(ring[1 - n], -1)
        if n == 3:
            (across,) = tie([across], [received[1]])
        if 1 < n < Z // 2:
            ring[n], ring[-n] = tie([ring[n], ring[-n]], [received[n - 2]])
        if n == 3:
            pieces = (packed, beside, across, swap(across, "co"))
            left = in_hbm(*prepare(OTHERS, meta, task_slots, pieces, PREPARE_COSTS[0]))
        if n == Z // 2:
            after = left[:1]
            apart = scatter(meta, ring[n], after, SELECT_COST[n])
            received.append([send(x, r) for r, x in enumerate(apart)])
            break
        outgoing = select(meta, [ring[o] for o in offsets], after, SELECT_COST[n])
        if n == 0:
            packed = pack(integrals, outgoing)
            across, beside = swap(packed, "xl"), swap(packed, "co")
        chosen.append(outgoing)
        received.append(exchange(outgoing, mirrored))

    mirrored = [received[n] for n in (1, 2, 0)]
    other = steps(meta, mirrored, (0, 512, 1024), 1, left, OTHER_COST)
    pieces = (*tie([pieces[0]], [other]), *pieces[1:])
    other = swap(other, "xl")
    left = in_hbm(*prepare(OWNS, meta, task_slots, pieces, PREPARE_COSTS[1]))
    return last(meta, received[4], received[3], mirrored, left, other, amplitudes, row_gap[None, :], column_gap[None, :])


def solution(mesh):
    fine = Mesh(mesh.devices.reshape(Z, XH, Y, XL, CO), ("z", "xh", "y", "xl", "co"))
    wide, narrow = ("z", "xh", "y"), ("xl", "co")
    return jax.shard_map(
        body,
        mesh=fine,
        in_specs=(P(narrow, wide), P(wide, narrow, None, None), P(wide, None), P(wide, None), P(wide), P(narrow)),
        out_specs=(P(narrow, wide), P(narrow, wide)),
        check_vma=False,
    )
```
